256 devices in a mesh: ctx: 128 (over z, y, x), head: 2 (over core).
Axes of the slice: x: 4, y: 4, z: 8, core: 2. Of those that a mesh axis runs over, the one named last changes fastest.
Arguments:
- queries: bfloat16 [32768, 3072], P(('ctx', 'head')), may hold values from -30 to 30
- keys: bfloat16 [32768, 3072], P(('ctx', 'head')), may hold values from -30 to 30
- values: bfloat16 [32768, 3072], P(('ctx', 'head')), may hold values from -6 to 6
- clip_ids: int32 [32768], P('ctx'), may hold values from 0 to 63, never falling along the last dimension, each value on 1 to 1024 neighbouring positions
- group_ids: int32 [32768], P('ctx'), may hold values from 0 to 511, never falling along the last dimension, each value on 1 to 128 neighbouring positions
- pair_kinds: int32 [128, 4], P('ctx'), may hold values from 0 to 2, as said below
Outputs:
- attended: bfloat16 [32768, 3072], P(('ctx', 'head'))
The draws below stay inside these ranges and needn't reach their ends.
Inputs may be any that keep to these rules, and one draw needn't show every extreme that they name: `pair_kinds`: entries are 0 (block not read), 1 (same clip, earlier or equal group) or 2 (every key of the block).
All inputs are finite; a program needn't handle non-finite values.
Results may differ from the reference program's by a relative error of at most 0.009.
Values may be sent and summed in bfloat16 or wider, within the bound.
A program may use at most 64 MiB of HBM per device.

```python
import math
import jax
import jax.numpy as jnp
import numpy as np
from jax import lax

BLK = 256
H = 24
HD = 128
WIN = 4
NBLK = 128
TOKENS = 32768
CLIPS = 64
GROUPS = 512


def listed_kinds(source):
    key = jax.random.fold_in(source, 7)
    listed_count = jax.random.randint(jax.random.fold_in(key, 1), (NBLK,), 0, WIN + 1)
    listed_count = listed_count.at[NBLK - 1].set(WIN)
    kind_code = jax.random.randint(jax.random.fold_in(key, 2), (NBLK, WIN), 1, 3)
    offsets = jnp.arange(1, WIN + 1, dtype=jnp.int32)
    listed = offsets[None, :] <= listed_count[:, None]
    return jnp.where(listed, kind_code, 0).astype(jnp.int32)


def draw_queries(key, part):
    key = jax.random.fold_in(key, 1)
    drawn = jax.random.truncated_normal(key, -6.0, 6.0, (TOKENS, H * HD), jnp.float32)
    return drawn.astype(jnp.bfloat16)


def draw_keys(key, part):
    key = jax.random.fold_in(key, 2)
    drawn = jax.random.truncated_normal(key, -6.0, 6.0, (TOKENS, H * HD), jnp.float32)
    return drawn.astype(jnp.bfloat16)


def draw_pair_kinds(key, part):
    drawn = listed_kinds(key)
    return drawn


def block_levels(rng, dims, pieces, least, top_value):
    def one(position, shards_of):
        draws = jax.random.uniform(jax.random.fold_in(jax.random.fold_in(rng, 6), position), (shards_of,), jnp.float32, least / len(pieces), top_value / len(pieces))
        return jnp.repeat(jnp.exp(draws), dims[position] // shards_of).reshape((-1,) + (1,) * (len(dims) - position - 1))

    level = one(*pieces[0])
    for cut in pieces[1:]:
        level = level * one(*cut)
    return level


def split_up(count, total, limit, skew):
    loads = [(1 << 20) // math.isqrt(rank ** skew) + 1 for rank in range(2, count + 1)]
    rest, counts = total - limit - (count - 1), [1] * (count - 1)
    while rest > 0:
        movable = [i for i in range(count - 1) if counts[i] < limit]
        mass, left = sum([loads[i] for i in movable]), rest
        for i in movable:
            more = min(limit - counts[i], max(1, left * loads[i] // mass), rest)
            counts[i] = counts[i] + more
            rest = rest - more
    return np.array([limit] + counts)


def ragged_sizes(rng, count, total, most, skew):
    if count == 2:
        one = jax.random.randint(rng, (), max(1, total - most), min(most, total - 1) + 1)
        return jnp.stack([one, total - one])
    tallies = jnp.asarray(split_up(count, total, most, skew), jnp.int32)
    pairs = (count - 1) // 2
    donor, taker = tallies[1:1 + 2 * pairs:2], tallies[2:2 + 2 * pairs:2]
    margin = jnp.minimum(donor - 1, most - taker)
    moved = jax.random.randint(jax.random.fold_in(rng, 1), (pairs,), 0, 1 << 20) % (margin + 1)
    tallies = tallies.at[1:1 + 2 * pairs:2].set(donor - moved).at[2:2 + 2 * pairs:2].set(taker + moved)
    return tallies[jax.random.permutation(jax.random.fold_in(rng, 2), count)]


def bell_draw(rng, shape, scale, most, split=(), kind=jnp.bfloat16):
    factor_of = block_levels(rng, shape, split, -0.22, 0.18) if split else 1.0
    result = jax.random.normal(rng, shape, jnp.float32) * scale * factor_of
    return jnp.minimum(jnp.maximum(result, -most), most).astype(kind)


def setup_inputs(seed: int = 0) -> dict:
    arg_keys = jax.random.split(jax.random.key(seed), 7)
    return {
        "queries": draw_queries(jax.random.fold_in(arg_keys[6], 71), 0),
        "keys": draw_keys(jax.random.fold_in(arg_keys[6], 71), 0),
        "values": bell_draw(arg_keys[2], (TOKENS, H * HD), 1.0, 6.0, ((0, 256),)),
        "clip_ids": jnp.searchsorted(jnp.cumsum(ragged_sizes(arg_keys[3], CLIPS, TOKENS, 4 * BLK, 1)), jnp.arange(TOKENS), side="right").astype(jnp.int32),
        "group_ids": jnp.searchsorted(jnp.cumsum(ragged_sizes(arg_keys[4], GROUPS, TOKENS, BLK // 2, 1)), jnp.arange(TOKENS), side="right").astype(jnp.int32),
        "pair_kinds": draw_pair_kinds(jax.random.fold_in(arg_keys[6], 71), 0),
    }


def reference(queries, keys, values, clip_ids, group_ids, pair_kinds):
    scale = HD ** -0.5
    padding = WIN * BLK
    width = (WIN + 1) * BLK
    key_padded = jnp.concatenate([jnp.zeros((padding, H * HD), keys.dtype), keys], axis=0)
    value_padded = jnp.concatenate([jnp.zeros((padding, H * HD), values.dtype), values], axis=0)
    clip_padded = jnp.concatenate([jnp.full((padding,), -1, jnp.int32), clip_ids.astype(jnp.int32)])
    group_padded = jnp.concatenate([jnp.full((padding,), -1, jnp.int32), group_ids.astype(jnp.int32)])
    distance = (WIN - jnp.arange(width, dtype=jnp.int32) // BLK).astype(jnp.int32)

    def attend_reader(block_index):
        start = (block_index * BLK).astype(jnp.int32)
        query_block = lax.dynamic_slice_in_dim(queries, start, BLK, 0).reshape(BLK, H, HD).astype(jnp.float32)
        key_block = lax.dynamic_slice_in_dim(key_padded, start, width, 0).reshape(width, H, HD).astype(jnp.float32)
        value_block = lax.dynamic_slice_in_dim(value_padded, start, width, 0).reshape(width, H, HD).astype(jnp.float32)
        key_clip = lax.dynamic_slice_in_dim(clip_padded, start, width, 0)
        key_group = lax.dynamic_slice_in_dim(group_padded, start, width, 0)
        query_clip = lax.dynamic_slice_in_dim(clip_ids.astype(jnp.int32), start, BLK, 0)
        query_group = lax.dynamic_slice_in_dim(group_ids.astype(jnp.int32), start, BLK, 0)
        kind_listed = lax.dynamic_index_in_dim(pair_kinds.astype(jnp.int32), block_index, 0, keepdims=False)
        kind_row = jnp.concatenate([kind_listed[::-1], jnp.ones((1,), jnp.int32)])
        kind_code = jnp.repeat(kind_row, BLK)
        valid = (block_index - distance) >= 0
        same_clip = (query_clip[:, None] == key_clip[None, :]) & (key_group[None, :] <= query_group[:, None])
        allowed = valid[None, :] & ((kind_code[None, :] == 2) | ((kind_code[None, :] == 1) & same_clip))
        scores = jnp.einsum("qhd,khd->hqk", query_block, key_block) * scale
        scores = jnp.where(allowed[None], scores, -1e30)
        highest = jnp.max(scores, axis=-1, keepdims=True)
        weights = jnp.where(allowed[None], jnp.exp(scores - highest), 0.0)
        row_total = jnp.sum(weights, axis=-1)
        rounded = weights.astype(jnp.bfloat16)
        rounded = lax.optimization_barrier(rounded).astype(jnp.float32)
        output = jnp.einsum("hqk,khd->qhd", rounded, value_block) / jnp.transpose(row_total)[:, :, None]
        return output.reshape(BLK, H * HD).astype(jnp.bfloat16)

    blocks = lax.map(attend_reader, jnp.arange(NBLK, dtype=jnp.int32))
    return blocks.reshape(TOKENS, H * HD)
```

```python
import jax
import jax.numpy as jnp
from jax import lax
from jax.experimental import pallas as pl
from jax.experimental.pallas import tpu as pltpu
from jax.sharding import PartitionSpec as P

HD = 128
WIN = 4
BLK = 256
SHARE = 128
ROW = 4
TEAM = 2 * ROW
HEADS = 3
SPAN = ROW * BLK
WINDOW = (WIN + 1) * BLK
MESH = pl.DeviceIdType.MESH
LOG2E = 1.4426950408889634
MASKED = -1e30


def kernel(q_ref, k_ref, v_ref, clip_ref, group_ref, kinds_ref, o_ref,
           mine, table, kv, qb, ob, bias,
           id_send, id_recv, idf_send, idf_recv, x_send, x_recv, q_send, q_recv, y_send, y_recv, o_send, o_recv):
    ctx = lax.axis_index("ctx")
    core = lax.axis_index("head")
    x = ctx % ROW
    me = 2 * x + core
    base = ctx - x
    has_next = ctx < 128 - ROW
    has_prev = ctx >= ROW

    def device(place):
        return (base + place // 2, place % 2)

    after, before = (ctx + ROW, core), (ctx - ROW, core)
    partners = [(me + step) % TEAM for step in (2, 6, 4, 3, 7, 5, 1)]

    barrier = pltpu.get_barrier_semaphore()
    for place in partners:
        pl.semaphore_signal(barrier, inc=1, device_id=device(place), device_id_type=MESH)

    @pl.when(has_next)
    def _():
        pl.semaphore_signal(barrier, inc=1, device_id=after, device_id_type=MESH)

    @pl.when(has_prev)
    def _():
        pl.semaphore_signal(barrier, inc=1, device_id=before, device_id_type=MESH)

    mine[0:1] = clip_ref[...]
    mine[1:2] = group_ref[...]
    for d in range(WIN):
        mine[2 + d:3 + d] = jnp.full((1, BLK), kinds_ref[0, d], jnp.int32)
    mine[6:8] = jnp.zeros((2, BLK), jnp.int32)

    @pl.when(jnp.logical_not(has_prev))
    def _():
        kv[:, :, 0:SPAN, :] = jnp.zeros((2, HEADS, SPAN, HD), jnp.bfloat16)
        table[0:ROW] = jnp.zeros((ROW, 8, BLK), jnp.int32)

    pl.semaphore_wait(barrier, TEAM - 1 + jnp.where(has_next, 1, 0) + jnp.where(has_prev, 1, 0))

    id_copies = []
    for n, step in enumerate((2, 6, 4)):
        id_copies.append(pltpu.make_async_remote_copy(
            mine, table.at[ROW + x], id_send.at[n], id_recv.at[n],
            device_id=device((me + step) % TEAM), device_id_type=MESH))
        id_copies[-1].start()
    own_ids = pltpu.make_async_copy(mine, table.at[ROW + x], id_recv.at[3])
    own_ids.start()

    def share(ref, h, landing, send, recv):
        def columns(place):
            return pl.ds(pl.multiple_of(HD * (HEADS * place + h), HD), HD)

        rows = pl.ds(pl.multiple_of(SHARE * me, SHARE), SHARE)
        for place in partners:
            pltpu.make_async_remote_copy(
                ref.at[:, columns(place)], landing.at[rows], send, recv,
                device_id=device(place), device_id_type=MESH).start()
        pltpu.make_async_copy(ref.at[:, columns(me)], landing.at[rows], recv).start()

    own = pl.ds(SPAN, SPAN)
    for h in range(HEADS):
        share(k_ref, h, kv.at[0, h, own], x_send.at[0, h], x_recv.at[0, h])
        share(v_ref, h, kv.at[1, h, own], x_send.at[1, h], x_recv.at[1, h])
        share(q_ref, h, qb.at[h], q_send.at[h], q_recv.at[h])

    def await_bytes(ref, sem):
        pltpu.make_async_copy(ref, ref, sem).wait()

    def forward(t, h):
        return pltpu.make_async_remote_copy(
            kv.at[t, h, own], kv.at[t, h, pl.ds(0, SPAN)], y_send.at[t, h], y_recv.at[t, h],
            device_id=after, device_id_type=MESH)

    def pass_on(h):
        for t in range(2):
            await_bytes(kv.at[t, h, own], x_recv.at[t, h])

            @pl.when(has_next)
            def _():
                forward(t, h).start()

    def table_forward():
        return pltpu.make_async_remote_copy(
            table.at[pl.ds(ROW, ROW)], table.at[pl.ds(0, ROW)], idf_send, idf_recv,
            device_id=after, device_id_type=MESH)

    for copy in id_copies:
        copy.wait()
    own_ids.wait()

    @pl.when(has_next)
    def _():
        table_forward().start()

    pass_on(0)

    @pl.when(has_prev)
    def _():
        table_forward().wait_recv()

    def build(i, carry):
        about = table[ROW + i]
        column = jnp.transpose(about.astype(jnp.float32))
        query_clip, query_group = column[:, 0:1], column[:, 1:2]
        for w in range(WIN + 1):
            there = table[i + w].astype(jnp.float32)
            allowed = (there[0:1] == query_clip) & (there[1:2] <= query_group)
            if w < WIN:
                kind = about[2 + WIN - 1 - w:3 + WIN - 1 - w]
                kind = jnp.where(has_prev | (i + w >= ROW), kind, 0)
                allowed = (kind == 2) | ((kind == 1) & allowed)
            bias[i, :, w * BLK:(w + 1) * BLK] = jnp.where(allowed, 0.0, MASKED)
        return carry

    lax.fori_loop(0, ROW, build, 0)

    def attend(h):
        def block(i, carry):
            start = pl.multiple_of(i * BLK, BLK)
            rows = qb[h, pl.ds(start, BLK)]
            keys = kv[0, h, pl.ds(start, WINDOW)]
            scores = lax.dot_general(rows, keys, (((1,), (1,)), ((), ())), preferred_element_type=jnp.float32)
            scores = scores + bias[i]
            highest = jnp.max(scores, axis=1, keepdims=True)
            weights = jnp.exp2((scores - highest) * (LOG2E * HD ** -0.5))
            total = jnp.sum(weights, axis=1, keepdims=True)
            out = jnp.dot(weights.astype(jnp.bfloat16), kv[1, h, pl.ds(start, WINDOW)], preferred_element_type=jnp.float32)
            ob[h, pl.ds(start, BLK)] = (out / total).astype(jnp.bfloat16)
            return carry

        lax.fori_loop(0, ROW, block, 0)

    def give_back(h):
        columns = pl.ds(pl.multiple_of(HD * (HEADS * me + h), HD), HD)
        for place in partners:
            pltpu.make_async_remote_copy(
                ob.at[h, pl.ds(pl.multiple_of(SHARE * place, SHARE), SHARE)], o_ref.at[:, columns],
                o_send.at[h], o_recv.at[h], device_id=device(place), device_id_type=MESH).start()
        pltpu.make_async_copy(
            ob.at[h, pl.ds(pl.multiple_of(SHARE * me, SHARE), SHARE)], o_ref.at[:, columns], o_recv.at[h]).start()

    for h in range(HEADS):
        if h + 1 < HEADS:
            pass_on(h + 1)
        await_bytes(qb.at[h], q_recv.at[h])

        @pl.when(has_prev)
        def _():
            forward(0, h).wait_recv()
            forward(1, h).wait_recv()

        attend(h)
        give_back(h)

    sent = (TEAM - 1) * SHARE
    for h in range(HEADS):
        for t in range(2):
            await_bytes(kv.at[t, h, pl.ds(0, sent)], x_send.at[t, h])

            @pl.when(has_next)
            def _():
                forward(t, h).wait_send()

        await_bytes(qb.at[h, pl.ds(0, sent)], q_send.at[h])

    @pl.when(has_next)
    def _():
        table_forward().wait_send()

    for h in range(HEADS):
        await_bytes(qb.at[h, pl.ds(0, sent)], o_send.at[h])
        await_bytes(qb.at[h], o_recv.at[h])


def shards(queries, keys, values, clip_ids, group_ids, pair_kinds):
    hbm = pl.BlockSpec(memory_space=pl.ANY)
    vmem = pl.BlockSpec(memory_space=pltpu.VMEM)
    dma = pltpu.SemaphoreType.DMA
    return pl.pallas_call(
        kernel,
        out_shape=jax.ShapeDtypeStruct(queries.shape, jnp.bfloat16),
        in_specs=[hbm, hbm, hbm, vmem, vmem, pl.BlockSpec(memory_space=pltpu.SMEM)],
        out_specs=hbm,
        scratch_shapes=[
            pltpu.VMEM((8, BLK), jnp.int32),
            pltpu.VMEM((2 * ROW, 8, BLK), jnp.int32),
            pltpu.VMEM((2, HEADS, 2 * SPAN, HD), jnp.bfloat16),
            pltpu.VMEM((HEADS, SPAN, HD), jnp.bfloat16),
            pltpu.VMEM((HEADS, SPAN, HD), jnp.bfloat16),
            pltpu.VMEM((ROW, BLK, WINDOW), jnp.float32),
            dma((3,)), dma((4,)), dma, dma,
            dma((2, HEADS)), dma((2, HEADS)), dma((HEADS,)), dma((HEADS,)),
            dma((2, HEADS)), dma((2, HEADS)), dma((HEADS,)), dma((HEADS,)),
        ],
        compiler_params=pltpu.CompilerParams(
            collective_id=0, has_side_effects=True, vmem_limit_bytes=60 * 1024 * 1024),
    )(queries, keys, values, clip_ids.reshape(1, BLK), group_ids.reshape(1, BLK), pair_kinds)


def solution(mesh):
    tokens = P(("ctx", "head"), None)
    return jax.shard_map(
        shards, mesh=mesh, in_specs=(tokens, tokens, tokens, P("ctx"), P("ctx"), P("ctx", None)),
        out_specs=tokens, check_vma=False)
```

```python
import jax
import jax.numpy as jnp
from jax import lax
from jax.experimental import pallas as pl
from jax.experimental.pallas import tpu as pltpu
from jax.sharding import PartitionSpec as P

HD = 128
WIN = 4
BLK = 256
SHARE = 128
ROW = 4
TEAM = 2 * ROW
HEADS = 3
SPAN = ROW * BLK
WINDOW = (WIN + 1) * BLK
BACK = 2
BACKED = BACK * BLK
MESH = pl.DeviceIdType.MESH
FACTOR = 1.4426950408889634 * HD ** -0.5
MASKED = -1e30


def kernel(q_ref, k_ref, v_ref, clip_ref, group_ref, kinds_ref, o_ref,
           mine, table, kv, qb, ob, qn, on, sn, op, sp, bias_a, bias_b, bias_n,
           tops, totals, outs, weights_a, weights_b,
           id_send, id_recv, idf_send, idf_recv, idb_send, idb_recv, x_send, x_recv, q_send, q_recv, y_send, y_recv,
           qb_send, qb_recv, p_send, p_recv, s_send, s_recv, o_send, o_recv):
    ctx = lax.axis_index("ctx")
    core = lax.axis_index("head")
    x = ctx % ROW
    me = 2 * x + core
    base = ctx - x
    has_next = ctx < 128 - ROW
    has_prev = ctx >= ROW

    def device(place):
        return (base + place // 2, place % 2)

    after, before = (ctx + ROW, core), (ctx - ROW, core)
    partners = [(me + step) % TEAM for step in (2, 6, 4, 3, 7, 5, 1)]

    barrier = pltpu.get_barrier_semaphore()
    for place in partners:
        pl.semaphore_signal(barrier, inc=1, device_id=device(place), device_id_type=MESH)

    @pl.when(has_next)
    def _():
        pl.semaphore_signal(barrier, inc=1, device_id=after, device_id_type=MESH)

    @pl.when(has_prev)
    def _():
        pl.semaphore_signal(barrier, inc=1, device_id=before, device_id_type=MESH)

    mine[0:1] = clip_ref[...]
    mine[1:2] = group_ref[...]
    for d in range(WIN):
        mine[2 + d:3 + d] = jnp.full((1, BLK), kinds_ref[0, d], jnp.int32)
    mine[6:8] = jnp.zeros((2, BLK), jnp.int32)

    @pl.when(jnp.logical_not(has_prev))
    def _():
        kv[:, :, BACKED:SPAN, :] = jnp.zeros((2, HEADS, SPAN - BACKED, HD), jnp.bfloat16)
        table[0:ROW] = jnp.zeros((ROW, 8, BLK), jnp.int32)
        op[...] = jnp.zeros((HEADS, BACKED, HD), jnp.bfloat16)
        sp[...] = jnp.full((HEADS, BACK, 8, BLK), MASKED, jnp.float32)

    pl.semaphore_wait(barrier, TEAM - 1 + jnp.where(has_next, 1, 0) + jnp.where(has_prev, 1, 0))

    id_copies = []
    for n, step in enumerate((2, 6, 4)):
        id_copies.append(pltpu.make_async_remote_copy(
            mine, table.at[ROW + x], id_send.at[n], id_recv.at[n],
            device_id=device((me + step) % TEAM), device_id_type=MESH))
        id_copies[-1].start()
    own_ids = pltpu.make_async_copy(mine, table.at[ROW + x], id_recv.at[3])
    own_ids.start()

    def share(ref, h, landing, send, recv):
        def columns(place):
            return pl.ds(pl.multiple_of(HD * (HEADS * place + h), HD), HD)

        rows = pl.ds(pl.multiple_of(SHARE * me, SHARE), SHARE)
        for place in partners:
            pltpu.make_async_remote_copy(
                ref.at[:, columns(place)], landing.at[rows], send, recv,
                device_id=device(place), device_id_type=MESH).start()
        pltpu.make_async_copy(ref.at[:, columns(me)], landing.at[rows], recv).start()

    own = pl.ds(SPAN, SPAN)

    def share_key(h):
        share(k_ref, h, kv.at[0, h, own], x_send.at[0, h], x_recv.at[0, h])

    def share_value(h):
        share(v_ref, h, kv.at[1, h, own], x_send.at[1, h], x_recv.at[1, h])

    def share_query(h, part):
        @pl.when(x // BACK == part)
        def _():
            share(q_ref, h, qb.at[h], q_send.at[h], q_recv.at[part, h])

    for h in range(HEADS):
        share_query(h, 0)
        share_key(h)
        share_value(h)
    for h in range(HEADS):
        share_query(h, 1)

    def await_bytes(ref, sem):
        pltpu.make_async_copy(ref, ref, sem).wait()

    def remote(src, dst, send, recv, to):
        return pltpu.make_async_remote_copy(src, dst, send, recv, device_id=to, device_id_type=MESH)

    def forward(t, h):
        return remote(kv.at[t, h, pl.ds(SPAN + BACKED, SPAN - BACKED)], kv.at[t, h, pl.ds(BACKED, SPAN - BACKED)],
                      y_send.at[t, h], y_recv.at[t, h], after)

    def backward(h):
        return remote(qb.at[h, pl.ds(0, BACKED)], qn.at[h], qb_send.at[h], qb_recv.at[h], before)

    def partial_out(h):
        return remote(on.at[h], op.at[h], p_send.at[h], p_recv.at[h], after)

    def partial_stats(h):
        return remote(sn.at[h], sp.at[h], s_send.at[h], s_recv.at[h], after)

    def table_forward():
        return remote(table.at[pl.ds(ROW, ROW)], table.at[pl.ds(0, ROW)], idf_send, idf_recv, after)

    def table_backward():
        return remote(table.at[pl.ds(ROW, ROW)], table.at[pl.ds(2 * ROW, ROW)], idb_send, idb_recv, before)

    def when(condition, *actions):
        @pl.when(condition)
        def _():
            for action in actions:
                action()

    def pass_on(t, h):
        await_bytes(kv.at[t, h, own], x_recv.at[t, h])
        when(has_next, lambda: forward(t, h).start())

    def pass_back(h):
        await_bytes(qb.at[h, pl.ds(0, BACKED)], q_recv.at[0, h])
        when(has_prev, lambda: backward(h).start())

    for copy in id_copies:
        copy.wait()
    own_ids.wait()
    when(has_next, lambda: table_forward().start())
    when(has_prev, lambda: table_backward().start())

    def pair(query_slot, key_slot):
        d = query_slot - key_slot
        if d < 0 or d > WIN:
            return jnp.full((BLK, BLK), MASKED, jnp.float32)
        about = table[query_slot]
        column = jnp.transpose(about.astype(jnp.float32))
        there = table[key_slot].astype(jnp.float32)
        allowed = (there[0:1] == column[:, 0:1]) & (there[1:2] <= column[:, 1:2])
        if d:
            kind = about[1 + d:2 + d]
            if key_slot < ROW:
                kind = jnp.where(has_prev, kind, 0)
            allowed = (kind == 2) | ((kind == 1) & allowed)
        return jnp.where(allowed, 0.0, MASKED)

    def terms(ref, i, query_slot, slots):
        for n, slot in enumerate(slots):
            ref[i, :, n * BLK:(n + 1) * BLK] = pair(query_slot, slot)

    def weigh(queries, keys, term):
        scores = lax.dot_general(queries, keys, (((1,), (1,)), ((), ())), preferred_element_type=jnp.float32)
        scores = scores + term
        highest = jnp.max(scores, axis=1, keepdims=True)
        weights = jnp.exp2((scores - highest) * FACTOR)
        return highest, jnp.sum(weights, axis=1, keepdims=True), weights.astype(jnp.bfloat16)

    def blend(weights, values):
        return jnp.dot(weights, values, preferred_element_type=jnp.float32)

    def block(i):
        return pl.ds(pl.multiple_of(i * BLK, BLK), BLK)

    def loop(body):
        def step(i, carry):
            body(i)
            return carry

        lax.fori_loop(0, BACK, step, 0)

    near = pl.ds(SPAN, BACKED)
    front = pl.ds(BACKED, SPAN)

    def partial(h):
        def body(i):
            highest, total, weights = weigh(qn[h, block(i)], kv[0, h, near], bias_n[i])
            on[h, block(i)] = blend(weights, kv[1, h, near]).astype(jnp.bfloat16)
            lane = lax.broadcasted_iota(jnp.int32, (BLK, HD), 1)
            sn[h, i] = jnp.transpose(jnp.where(lane == 0, highest, total))[0:8]

        loop(body)
        partial_out(h).start()
        partial_stats(h).start()

    def give_back(h, i):
        columns = pl.ds(pl.multiple_of(HD * (HEADS * me + h), HD), HD)
        for place in (2 * i, 2 * i + 1):
            rows = ob.at[h, pl.ds(pl.multiple_of(SHARE * place, SHARE), SHARE)]

            @pl.when(me != place)
            def _():
                remote(rows, o_ref.at[:, columns], o_send.at[h], o_recv.at[h], device(place)).start()

            @pl.when(me == place)
            def _():
                pltpu.make_async_copy(rows, o_ref.at[:, columns], o_recv.at[h]).start()

    def weigh_first(h):
        def body(i):
            tops[i], totals[i], weights_a[i] = weigh(qb[h, block(i)], kv[0, h, front], bias_a[i])

        loop(body)

    def blend_first(h):
        def body(i):
            outs[i] = blend(weights_a[i], kv[1, h, front])

        loop(body)

    def merge(h):
        def body(i):
            stats = jnp.transpose(sp[h, i])
            highest, other = tops[i], stats[:, 0:1]
            top = jnp.maximum(highest, other)
            here, there = jnp.exp2((highest - top) * FACTOR), jnp.exp2((other - top) * FACTOR)
            total = totals[i] * here + stats[:, 1:2] * there
            out = outs[i] * here + op[h, block(i)].astype(jnp.float32) * there
            ob[h, block(i)] = (out / total).astype(jnp.bfloat16)
            give_back(h, i)

        loop(body)

    def weigh_last(h):
        def body(i):
            _, totals[BACK + i], weights_b[i] = weigh(
                qb[h, block(BACK + i)], kv[0, h, pl.ds(pl.multiple_of((BACK + i) * BLK, BLK), WINDOW)], bias_b[i])

        loop(body)

    def blend_last(h):
        def body(i):
            out = blend(weights_b[i], kv[1, h, pl.ds(pl.multiple_of((BACK + i) * BLK, BLK), WINDOW)])
            ob[h, block(BACK + i)] = (out / totals[BACK + i]).astype(jnp.bfloat16)
            give_back(h, BACK + i)

        loop(body)

    def await_keys(h):
        when(has_prev, lambda: forward(0, h).wait_recv())

    def await_values(h):
        when(has_prev, lambda: forward(1, h).wait_recv())

    def await_last(h):
        await_bytes(qb.at[h, pl.ds(BACKED, SPAN - BACKED)], q_recv.at[1, h])

    def await_partial(h):
        when(has_prev, lambda: partial_out(h).wait_recv(), lambda: partial_stats(h).wait_recv())

    def next_part(h):
        @pl.when(has_next)
        def _():
            backward(h).wait_recv()
            partial(h)

    pass_back(0)
    pass_on(0, 0)
    when(has_next, lambda: table_backward().wait_recv())

    @pl.when(has_next)
    def _():
        for i in range(BACK):
            terms(bias_n, i, 2 * ROW + i, range(ROW, ROW + BACK))

    pass_on(1, 0)
    next_part(0)
    pass_back(1)
    when(has_prev, lambda: table_forward().wait_recv())
    for i in range(BACK):
        terms(bias_a, i, ROW + i, range(BACK, BACK + ROW))
    pass_on(0, 1)
    await_keys(0)
    weigh_first(0)
    await_values(0)
    blend_first(0)
    pass_on(1, 1)
    next_part(1)
    pass_back(2)
    await_partial(0)
    merge(0)
    for i in range(BACK):
        terms(bias_b, i, ROW + BACK + i, range(BACK + i, BACK + i + WIN + 1))
    pass_on(0, 2)
    await_keys(1)
    weigh_first(1)
    pass_on(1, 2)
    next_part(2)
    await_values(1)
    blend_first(1)
    await_last(0)
    weigh_last(0)
    blend_last(0)
    await_partial(1)
    merge(1)
    await_last(1)
    weigh_last(1)
    blend_last(1)
    await_keys(2)
    weigh_first(2)
    await_last(2)
    weigh_last(2)
    await_values(2)
    blend_first(2)
    blend_last(2)
    await_partial(2)
    merge(2)

    sent = (TEAM - 1) * SHARE
    for h in range(HEADS):
        for t in range(2):
            await_bytes(kv.at[t, h, pl.ds(0, sent)], x_send.at[t, h])
        await_bytes(qb.at[h, pl.ds(0, sent)], q_send.at[h])

    @pl.when(has_next)
    def _():
        table_forward().wait_send()
        for h in range(HEADS):
            forward(0, h).wait_send()
            forward(1, h).wait_send()
            partial_out(h).wait_send()
            partial_stats(h).wait_send()

    @pl.when(has_prev)
    def _():
        table_backward().wait_send()
        for h in range(HEADS):
            backward(h).wait_send()

    for h in range(HEADS):
        await_bytes(qb.at[h, pl.ds(0, sent)], o_send.at[h])
        await_bytes(qb.at[h], o_recv.at[h])


def shards(queries, keys, values, clip_ids, group_ids, pair_kinds):
    hbm = pl.BlockSpec(memory_space=pl.ANY)
    vmem = pl.BlockSpec(memory_space=pltpu.VMEM)
    dma = pltpu.SemaphoreType.DMA
    bf16 = jnp.bfloat16
    return pl.pallas_call(
        kernel,
        out_shape=jax.ShapeDtypeStruct(queries.shape, bf16),
        in_specs=[hbm, hbm, hbm, vmem, vmem, pl.BlockSpec(memory_space=pltpu.SMEM)],
        out_specs=hbm,
        scratch_shapes=[
            pltpu.VMEM((8, BLK), jnp.int32),
            pltpu.VMEM((3 * ROW, 8, BLK), jnp.int32),
            pltpu.VMEM((2, HEADS, 2 * SPAN, HD), bf16),
            pltpu.VMEM((HEADS, SPAN, HD), bf16),
            pltpu.VMEM((HEADS, SPAN, HD), bf16),
            pltpu.VMEM((HEADS, BACKED, HD), bf16),
            pltpu.VMEM((HEADS, BACKED, HD), bf16),
            pltpu.VMEM((HEADS, BACK, 8, BLK), jnp.float32),
            pltpu.VMEM((HEADS, BACKED, HD), bf16),
            pltpu.VMEM((HEADS, BACK, 8, BLK), jnp.float32),
            pltpu.VMEM((BACK, BLK, SPAN), jnp.float32),
            pltpu.VMEM((BACK, BLK, WINDOW), jnp.float32),
            pltpu.VMEM((BACK, BLK, BACKED), jnp.float32),
            pltpu.VMEM((BACK, BLK, 1), jnp.float32),
            pltpu.VMEM((ROW, BLK, 1), jnp.float32),
            pltpu.VMEM((BACK, BLK, HD), jnp.float32),
            pltpu.VMEM((BACK, BLK, SPAN), bf16),
            pltpu.VMEM((BACK, BLK, WINDOW), bf16),
            dma((3,)), dma((4,)), dma, dma, dma, dma,
            dma((2, HEADS)), dma((2, HEADS)), dma((HEADS,)), dma((2, HEADS)),
            dma((2, HEADS)), dma((2, HEADS)), dma((HEADS,)), dma((HEADS,)),
            dma((HEADS,)), dma((HEADS,)), dma((HEADS,)), dma((HEADS,)), dma((HEADS,)), dma((HEADS,)),
        ],
        compiler_params=pltpu.CompilerParams(
            collective_id=0, has_side_effects=True, vmem_limit_bytes=60 * 1024 * 1024),
    )(queries, keys, values, clip_ids.reshape(1, BLK), group_ids.reshape(1, BLK), pair_kinds)


def solution(mesh):
    tokens = P(("ctx", "head"), None)
    return jax.shard_map(
        shards, mesh=mesh, in_specs=(tokens, tokens, tokens, P("ctx"), P("ctx"), P("ctx", None)),
        out_specs=tokens, check_vma=False)
```

```python
import jax
import jax.numpy as jnp
from jax import lax
from jax.experimental import pallas as pl
from jax.experimental.pallas import tpu as pltpu
from jax.sharding import PartitionSpec as P

HD = 128
WIN = 4
BLK = 256
SHARE = 128
ROW = 4
TEAM = 2 * ROW
HEADS = 3
SPAN = ROW * BLK
WINDOW = (WIN + 1) * BLK
BACK = (0, 3, 3)
MOST = max(BACK)
SPLIT = tuple(h for h in range(HEADS) if BACK[h])
MESH = pl.DeviceIdType.MESH
FACTOR = 1.4426950408889634 * HD ** -0.5
MASKED = -1e30


def kernel(q_ref, k_ref, v_ref, clip_ref, group_ref, kinds_ref, o_ref,
           mine, table, kv, qb, ob, qn, on, sn, op, sp, bias, bias_n,
           tops, totals, outs, weights_a, weights_b,
           id_send, id_recv, idf_send, idf_recv, idb_send, idb_recv, x_send, x_recv, q_send, q_recv, y_send, y_recv,
           qb_send, qb_recv, p_send, p_recv, s_send, s_recv, o_send, o_recv):
    ctx = lax.axis_index("ctx")
    core = lax.axis_index("head")
    x = ctx % ROW
    me = 2 * x + core
    base = ctx - x
    has_next = ctx < 128 - ROW
    has_prev = ctx >= ROW

    def device(place):
        return (base + place // 2, place % 2)

    after, before = (ctx + ROW, core), (ctx - ROW, core)
    partners = [(me + step) % TEAM for step in (2, 6, 4, 3, 7, 5, 1)]

    barrier = pltpu.get_barrier_semaphore()
    for place in partners:
        pl.semaphore_signal(barrier, inc=1, device_id=device(place), device_id_type=MESH)

    @pl.when(has_next)
    def _():
        pl.semaphore_signal(barrier, inc=1, device_id=after, device_id_type=MESH)

    @pl.when(has_prev)
    def _():
        pl.semaphore_signal(barrier, inc=1, device_id=before, device_id_type=MESH)

    mine[0:1] = clip_ref[...]
    mine[1:2] = group_ref[...]
    for d in range(WIN):
        mine[2 + d:3 + d] = jnp.full((1, BLK), kinds_ref[0, d], jnp.int32)
    mine[6:8] = jnp.zeros((2, BLK), jnp.int32)

    @pl.when(jnp.logical_not(has_prev))
    def _():
        kv[:, :, 0:SPAN, :] = jnp.zeros((2, HEADS, SPAN, HD), jnp.bfloat16)
        table[0:ROW] = jnp.zeros((ROW, 8, BLK), jnp.int32)
        op[...] = jnp.zeros((HEADS, MOST * BLK, HD), jnp.bfloat16)
        sp[...] = jnp.full((HEADS, MOST, 8, BLK), MASKED, jnp.float32)

    pl.semaphore_wait(barrier, TEAM - 1 + jnp.where(has_next, 1, 0) + jnp.where(has_prev, 1, 0))

    id_copies = []
    for n, step in enumerate((2, 6, 4)):
        id_copies.append(pltpu.make_async_remote_copy(
            mine, table.at[ROW + x], id_send.at[n], id_recv.at[n],
            device_id=device((me + step) % TEAM), device_id_type=MESH))
        id_copies[-1].start()
    own_ids = pltpu.make_async_copy(mine, table.at[ROW + x], id_recv.at[3])
    own_ids.start()

    def share(ref, h, landing, send, recv):
        def columns(place):
            return pl.ds(pl.multiple_of(HD * (HEADS * place + h), HD), HD)

        rows = pl.ds(pl.multiple_of(SHARE * me, SHARE), SHARE)
        for place in partners:
            pltpu.make_async_remote_copy(
                ref.at[:, columns(place)], landing.at[rows], send, recv,
                device_id=device(place), device_id_type=MESH).start()
        pltpu.make_async_copy(ref.at[:, columns(me)], landing.at[rows], recv).start()

    own = pl.ds(SPAN, SPAN)

    def share_key(h):
        share(k_ref, h, kv.at[0, h, own], x_send.at[0, h], x_recv.at[0, h])

    def share_value(h):
        share(v_ref, h, kv.at[1, h, own], x_send.at[1, h], x_recv.at[1, h])

    def share_query(h):
        share(q_ref, h, qb.at[h], q_send.at[h], q_recv.at[h])

    share_key(0)
    share_value(0)
    for h in SPLIT:
        share_query(h)
        share_key(h)
        share_value(h)
    share_query(0)

    def await_bytes(ref, sem):
        pltpu.make_async_copy(ref, ref, sem).wait()

    def remote(src, dst, send, recv, to):
        return pltpu.make_async_remote_copy(src, dst, send, recv, device_id=to, device_id_type=MESH)

    def forward(t, h):
        first = BACK[h] * BLK
        return remote(kv.at[t, h, pl.ds(SPAN + first, SPAN - first)], kv.at[t, h, pl.ds(first, SPAN - first)],
                      y_send.at[t, h], y_recv.at[t, h], after)

    def backward(h):
        first = pl.ds(0, BACK[h] * BLK)
        return remote(qb.at[h, first], qn.at[h, first], qb_send.at[h], qb_recv.at[h], before)

    def partial_out(h, i):
        return remote(on.at[h, pl.ds(i * BLK, BLK)], op.at[h, pl.ds(i * BLK, BLK)],
                      p_send.at[h, i], p_recv.at[h, i], after)

    def partial_stats(h, i):
        return remote(sn.at[h, i], sp.at[h, i], s_send.at[h, i], s_recv.at[h, i], after)

    def table_forward():
        return remote(table.at[pl.ds(ROW, ROW)], table.at[pl.ds(0, ROW)], idf_send, idf_recv, after)

    def table_backward():
        return remote(table.at[pl.ds(ROW, ROW)], table.at[pl.ds(2 * ROW, ROW)], idb_send, idb_recv, before)

    def when(condition, *actions):
        @pl.when(condition)
        def _():
            for action in actions:
                action()

    def pass_on(t, h):
        await_bytes(kv.at[t, h, own], x_recv.at[t, h])
        when(has_next, lambda: forward(t, h).start())

    def pass_back(h):
        await_bytes(qb.at[h], q_recv.at[h])
        when(has_prev, lambda: backward(h).start())

    for copy in id_copies:
        copy.wait()
    own_ids.wait()
    when(has_next, lambda: table_forward().start())
    when(has_prev, lambda: table_backward().start())

    def pair(query_slot, key_slot):
        d = query_slot - key_slot
        if d < 0 or d > WIN:
            return jnp.full((BLK, BLK), MASKED, jnp.float32)
        about = table[query_slot]
        column = jnp.transpose(about.astype(jnp.float32))
        there = table[key_slot].astype(jnp.float32)
        allowed = (there[0:1] == column[:, 0:1]) & (there[1:2] <= column[:, 1:2])
        if d:
            kind = about[1 + d:2 + d]
            if key_slot < ROW:
                kind = jnp.where(has_prev, kind, 0)
            allowed = (kind == 2) | ((kind == 1) & allowed)
        return jnp.where(allowed, 0.0, MASKED)

    def terms(ref, i, query_slot, slots):
        for n, slot in enumerate(slots):
            ref[i, :, n * BLK:(n + 1) * BLK] = pair(query_slot, slot)

    def weigh(queries, keys, term):
        scores = lax.dot_general(queries, keys, (((1,), (1,)), ((), ())), preferred_element_type=jnp.float32)
        scores = scores + term
        highest = jnp.max(scores, axis=1, keepdims=True)
        weights = jnp.exp2((scores - highest) * FACTOR)
        return highest, jnp.sum(weights, axis=1, keepdims=True), weights.astype(jnp.bfloat16)

    def blend(weights, values):
        return jnp.dot(weights, values, preferred_element_type=jnp.float32)

    def block(i):
        return pl.ds(i * BLK if isinstance(i, int) else pl.multiple_of(i * BLK, BLK), BLK)

    def loop(count, body):
        def step(i, carry):
            body(i)
            return carry

        lax.fori_loop(0, count, step, 0)

    def window(i):
        return pl.ds(i * BLK if isinstance(i, int) else pl.multiple_of(i * BLK, BLK), WINDOW)

    def front(h, i):
        return pl.ds(BACK[h] * BLK, (ROW + 1 + i - BACK[h]) * BLK)

    def partial(h):
        for i in range(BACK[h]):
            rows = pl.ds(SPAN + i * BLK, (BACK[h] - i) * BLK)
            highest, total, weights = weigh(qn[h, block(i)], kv[0, h, rows], bias_n[i, :, 0:rows.size])
            on[h, block(i)] = blend(weights, kv[1, h, rows]).astype(jnp.bfloat16)
            lane = lax.broadcasted_iota(jnp.int32, (BLK, HD), 1)
            sn[h, i] = jnp.transpose(jnp.where(lane == 0, highest, total))[0:8]
            partial_out(h, i).start()
            partial_stats(h, i).start()

    def give_back(h, i):
        columns = pl.ds(pl.multiple_of(HD * (HEADS * me + h), HD), HD)
        for place in (2 * i, 2 * i + 1):
            rows = ob.at[h, pl.ds(pl.multiple_of(SHARE * place, SHARE), SHARE)]

            @pl.when(me != place)
            def _():
                remote(rows, o_ref.at[:, columns], o_send.at[h], o_recv.at[h], device(place)).start()

            @pl.when(me == place)
            def _():
                pltpu.make_async_copy(rows, o_ref.at[:, columns], o_recv.at[h]).start()

    def weigh_first(h):
        for i in range(BACK[h]):
            rows = front(h, i)
            tops[i], totals[i], weights_a[i, :, 0:rows.size] = weigh(
                qb[h, block(i)], kv[0, h, rows], bias[i, :, (BACK[h] - i) * BLK:])

    def blend_first(h):
        for i in range(BACK[h]):
            rows = front(h, i)
            outs[i] = blend(weights_a[i, :, 0:rows.size], kv[1, h, rows])

    def merge(h):
        for i in range(BACK[h]):
            when(has_prev, lambda: partial_out(h, i).wait_recv(), lambda: partial_stats(h, i).wait_recv())
            stats = jnp.transpose(sp[h, i])
            highest, other = tops[i], stats[:, 0:1]
            top = jnp.maximum(highest, other)
            here, there = jnp.exp2((highest - top) * FACTOR), jnp.exp2((other - top) * FACTOR)
            total = totals[i] * here + stats[:, 1:2] * there
            out = outs[i] * here + op[h, block(i)].astype(jnp.float32) * there
            ob[h, block(i)] = (out / total).astype(jnp.bfloat16)
            give_back(h, i)

    def weigh_last(h):
        for i in range(BACK[h], ROW):
            _, totals[i], weights_b[i - BACK[h]] = weigh(qb[h, block(i)], kv[0, h, window(i)], bias[i])

    def blend_last(h):
        for i in range(BACK[h], ROW):
            out = blend(weights_b[i - BACK[h]], kv[1, h, window(i)])
            ob[h, block(i)] = (out / totals[i]).astype(jnp.bfloat16)
            give_back(h, i)

    def attend(h):
        def body(i):
            _, total, weights = weigh(qb[h, block(i)], kv[0, h, window(i)], bias[i])
            out = blend(weights, kv[1, h, window(i)])
            ob[h, block(i)] = (out / total).astype(jnp.bfloat16)
            give_back(h, i)

        loop(ROW, body)

    def await_keys(h):
        when(has_prev, lambda: forward(0, h).wait_recv())

    def await_values(h):
        when(has_prev, lambda: forward(1, h).wait_recv())

    def await_queries(h):
        await_bytes(qb.at[h], q_recv.at[h])

    def next_part(h):
        @pl.when(has_next)
        def _():
            backward(h).wait_recv()
            partial(h)

    pass_on(0, 0)
    when(has_prev, lambda: table_forward().wait_recv())
    for i in range(ROW):
        terms(bias, i, ROW + i, range(i, ROW + i + 1))

    @pl.when(has_next)
    def _():
        table_backward().wait_recv()
        for i in range(MOST):
            terms(bias_n, i, 2 * ROW + i, range(ROW + i, ROW + MOST))

    pass_on(1, 0)
    pass_back(1)
    pass_on(0, 1)
    pass_on(1, 1)
    next_part(1)
    pass_back(2)
    pass_on(0, 2)
    await_keys(1)
    weigh_last(1)
    weigh_first(1)
    await_values(1)
    blend_last(1)
    blend_first(1)
    merge(1)
    pass_on(1, 2)
    next_part(2)
    await_keys(2)
    weigh_last(2)
    weigh_first(2)
    await_queries(0)
    await_keys(0)
    await_values(0)
    attend(0)
    await_values(2)
    blend_last(2)
    blend_first(2)
    merge(2)

    sent = (TEAM - 1) * SHARE
    for h in range(HEADS):
        for t in range(2):
            await_bytes(kv.at[t, h, pl.ds(0, sent)], x_send.at[t, h])
        await_bytes(qb.at[h, pl.ds(0, sent)], q_send.at[h])

    @pl.when(has_next)
    def _():
        table_forward().wait_send()
        for h in range(HEADS):
            forward(0, h).wait_send()
            forward(1, h).wait_send()
        for h in SPLIT:
            for i in range(BACK[h]):
                partial_out(h, i).wait_send()
                partial_stats(h, i).wait_send()

    @pl.when(has_prev)
    def _():
        table_backward().wait_send()
        for h in SPLIT:
            backward(h).wait_send()

    for h in range(HEADS):
        await_bytes(qb.at[h, pl.ds(0, sent)], o_send.at[h])
        await_bytes(qb.at[h], o_recv.at[h])


def shards(queries, keys, values, clip_ids, group_ids, pair_kinds):
    hbm = pl.BlockSpec(memory_space=pl.ANY)
    vmem = pl.BlockSpec(memory_space=pltpu.VMEM)
    dma = pltpu.SemaphoreType.DMA
    bf16 = jnp.bfloat16
    return pl.pallas_call(
        kernel,
        out_shape=jax.ShapeDtypeStruct(queries.shape, bf16),
        in_specs=[hbm, hbm, hbm, vmem, vmem, pl.BlockSpec(memory_space=pltpu.SMEM)],
        out_specs=hbm,
        scratch_shapes=[
            pltpu.VMEM((8, BLK), jnp.int32),
            pltpu.VMEM((3 * ROW, 8, BLK), jnp.int32),
            pltpu.VMEM((2, HEADS, 2 * SPAN, HD), bf16),
            pltpu.VMEM((HEADS, SPAN, HD), bf16),
            pltpu.VMEM((HEADS, SPAN, HD), bf16),
            pltpu.VMEM((HEADS, MOST * BLK, HD), bf16),
            pltpu.VMEM((HEADS, MOST * BLK, HD), bf16),
            pltpu.VMEM((HEADS, MOST, 8, BLK), jnp.float32),
            pltpu.VMEM((HEADS, MOST * BLK, HD), bf16),
            pltpu.VMEM((HEADS, MOST, 8, BLK), jnp.float32),
            pltpu.VMEM((ROW, BLK, WINDOW), jnp.float32),
            pltpu.VMEM((MOST, BLK, MOST * BLK), jnp.float32),
            pltpu.VMEM((MOST, BLK, 1), jnp.float32),
            pltpu.VMEM((ROW, BLK, 1), jnp.float32),
            pltpu.VMEM((MOST, BLK, HD), jnp.float32),
            pltpu.VMEM((MOST, BLK, SPAN), bf16),
            pltpu.VMEM((ROW - min(BACK[h] for h in SPLIT), BLK, WINDOW), bf16),
            dma((3,)), dma((4,)), dma, dma, dma, dma,
            dma((2, HEADS)), dma((2, HEADS)), dma((HEADS,)), dma((HEADS,)),
            dma((2, HEADS)), dma((2, HEADS)), dma((HEADS,)), dma((HEADS,)),
            dma((HEADS, MOST)), dma((HEADS, MOST)), dma((HEADS, MOST)), dma((HEADS, MOST)), dma((HEADS,)), dma((HEADS,)),
        ],
        compiler_params=pltpu.CompilerParams(
            collective_id=0, has_side_effects=True, vmem_limit_bytes=53 * 1024 * 1024),
    )(queries, keys, values, clip_ids.reshape(1, BLK), group_ids.reshape(1, BLK), pair_kinds)


def solution(mesh):
    tokens = P(("ctx", "head"), None)
    return jax.shard_map(
        shards, mesh=mesh, in_specs=(tokens, tokens, tokens, P("ctx"), P("ctx"), P("ctx", None)),
        out_specs=tokens, check_vma=False)
```

```python
import jax
import jax.numpy as jnp
from jax import lax
from jax.experimental import pallas as pl
from jax.experimental.pallas import tpu as pltpu
from jax.sharding import PartitionSpec as P

HD = 128
WIN = 4
BLK = 256
SHARE = 128
ROW = 4
TEAM = 2 * ROW
HEADS = 3
SPAN = ROW * BLK
WINDOW = (WIN + 1) * BLK
BACK = (0, 3, 2)
MOST = max(BACK)
SPLIT = tuple(h for h in range(HEADS) if BACK[h])
FIRST = (1, 0)
MESH = pl.DeviceIdType.MESH
FACTOR = 1.4426950408889634 * HD ** -0.5
MASKED = -1e30


def kernel(q_ref, k_ref, v_ref, clip_ref, group_ref, kinds_ref, o_ref,
           mine, table, kv, qb, ob, qn, on, sn, op, sp, bias, bias_n,
           tops, totals, outs, weights_of,
           id_send, id_recv, idf_send, idf_recv, idb_send, idb_recv, x_send, x_recv, q_send, q_recv, y_send, y_recv,
           chip_recv, qb_send, qb_recv, p_send, p_recv, s_send, s_recv, o_send, o_recv):
    ctx = lax.axis_index("ctx")
    core = lax.axis_index("head")
    x = ctx % ROW
    me = 2 * x + core
    base = ctx - x
    has_next = ctx < 128 - ROW
    has_prev = ctx >= ROW

    def device(place):
        return (base + place // 2, place % 2)

    after, before = (ctx + ROW, core), (ctx - ROW, core)

    def place_on(chips, c):
        return 2 * ((x + chips) % ROW) + c

    sibling = 2 * x + 1 - core
    partners = [place_on(chips, c) for c in (0, 1) for chips in (1, 2, 3)] + [sibling]

    barrier = pltpu.get_barrier_semaphore()
    for place in partners:
        pl.semaphore_signal(barrier, inc=1, device_id=device(place), device_id_type=MESH)

    @pl.when(has_next)
    def _():
        pl.semaphore_signal(barrier, inc=1, device_id=after, device_id_type=MESH)

    @pl.when(has_prev)
    def _():
        pl.semaphore_signal(barrier, inc=1, device_id=before, device_id_type=MESH)

    mine[0:1] = clip_ref[...]
    mine[1:2] = group_ref[...]
    for d in range(WIN):
        mine[2 + d:3 + d] = jnp.full((1, BLK), kinds_ref[0, d], jnp.int32)
    mine[6:8] = jnp.zeros((2, BLK), jnp.int32)

    for h in SPLIT:
        op[h, BACK[h] * BLK:] = jnp.zeros((SPAN - BACK[h] * BLK, HD), jnp.bfloat16)
        sp[h, BACK[h]:] = jnp.full((ROW - BACK[h], 8, BLK), MASKED, jnp.float32)

    @pl.when(jnp.logical_not(has_prev))
    def _():
        kv[:, :, 0:SPAN, :] = jnp.zeros((2, HEADS, SPAN, HD), jnp.bfloat16)
        table[0:ROW] = jnp.zeros((ROW, 8, BLK), jnp.int32)
        for h in SPLIT:
            op[h, 0:BACK[h] * BLK] = jnp.zeros((BACK[h] * BLK, HD), jnp.bfloat16)
            sp[h, 0:BACK[h]] = jnp.full((BACK[h], 8, BLK), MASKED, jnp.float32)

    pl.semaphore_wait(barrier, TEAM - 1 + jnp.where(has_next, 1, 0) + jnp.where(has_prev, 1, 0))

    id_copies = []
    for n, step in enumerate((2, 6, 4)):
        id_copies.append(pltpu.make_async_remote_copy(
            mine, table.at[ROW + x], id_send.at[n], id_recv.at[n],
            device_id=device((me + step) % TEAM), device_id_type=MESH))
        id_copies[-1].start()
    own_ids = pltpu.make_async_copy(mine, table.at[ROW + x], id_recv.at[3])
    own_ids.start()

    def remote(src, dst, send, recv, to):
        return pltpu.make_async_remote_copy(src, dst, send, recv, device_id=to, device_id_type=MESH)

    def share(ref, h, landing, send, recv, places):
        rows = pl.ds(pl.multiple_of(SHARE * me, SHARE), SHARE)
        for place in places:
            source = ref.at[:, pl.ds(pl.multiple_of(HD * (HEADS * place + h), HD), HD)]
            if place is me:
                pltpu.make_async_copy(source, landing.at[rows], recv).start()
            else:
                remote(source, landing.at[rows], send, recv, device(place)).start()

    own = pl.ds(SPAN, SPAN)
    here = (sibling, me)
    away = [place_on(chips, c) for c in FIRST for chips in (1, 3, 2)]
    everywhere = [*away, *here]

    def share_key(h, part, steps=everywhere):
        share(k_ref, h, kv.at[0, h, own], x_send.at[0, h], x_recv.at[0, h, part], steps)

    def share_value(h, part, steps=everywhere):
        share(v_ref, h, kv.at[1, h, own], x_send.at[1, h], x_recv.at[1, h, part], steps)

    def share_query(h, part):
        share(q_ref, h, qb.at[h], q_send.at[h], q_recv.at[h, part], everywhere)

    share_key(0, 0, here)
    share_value(0, 0, here)
    share_key(0, 1, away)
    share_value(0, 1, away)
    share(q_ref, 0, qb.at[0], q_send.at[0], chip_recv.at[0], here)
    for h in SPLIT:
        @pl.when(x < BACK[h])
        def _():
            share_query(h, 0)
            share_key(h, 0)
            share_value(h, 0)

        @pl.when(x >= BACK[h])
        def _():
            share_key(h, 1)
            share_value(h, 1)
            share_query(h, 1)

    for chips in (1, 3, 2):
        share(q_ref, 0, qb.at[0], q_send.at[0], chip_recv.at[chips], [place_on(chips, c) for c in FIRST])

    def await_bytes(ref, sem):
        pltpu.make_async_copy(ref, ref, sem).wait()

    def forward(t, h):
        first = BACK[h] * BLK
        return remote(kv.at[t, h, pl.ds(SPAN + first, SPAN - first)], kv.at[t, h, pl.ds(first, SPAN - first)],
                      y_send.at[t, h], y_recv.at[t, h], after)

    def forward_block(t, i):
        rows = pl.ds(pl.multiple_of(i * BLK, BLK), BLK)
        return remote(kv.at[t, 0, own].at[rows], kv.at[t, 0, rows], y_send.at[t, 0], y_recv.at[t, 0], after)

    def backward(h):
        first = pl.ds(0, BACK[h] * BLK)
        return remote(qb.at[h, first], qn.at[h, first], qb_send.at[h], qb_recv.at[h], before)

    def partial_out(h, i):
        return remote(on.at[h, pl.ds(i * BLK, BLK)], op.at[h, pl.ds(i * BLK, BLK)],
                      p_send.at[h, i], p_recv.at[h, i], after)

    def partial_stats(h, i):
        return remote(sn.at[h, i], sp.at[h, i], s_send.at[h, i], s_recv.at[h, i], after)

    def table_forward():
        return remote(table.at[pl.ds(ROW, ROW)], table.at[pl.ds(0, ROW)], idf_send, idf_recv, after)

    def table_backward():
        return remote(table.at[pl.ds(ROW, ROW)], table.at[pl.ds(2 * ROW, ROW)], idb_send, idb_recv, before)

    def when(condition, *actions):
        @pl.when(condition)
        def _():
            for action in actions:
                action()

    def first_rows(h):
        return pl.ds(0, BACK[h] * BLK)

    def last_rows(h):
        return pl.ds(BACK[h] * BLK, SPAN - BACK[h] * BLK)

    def pass_on(t, h):
        await_bytes(kv.at[t, h, last_rows(h)], x_recv.at[t, h, 1])
        when(has_next, lambda: forward(t, h).start())

    def pass_own(t):
        await_bytes(kv.at[t, 0, pl.ds(0, BLK)], x_recv.at[t, 0, 0])
        when(has_next, lambda: forward_block(t, x).start())

    def pass_rest(t):
        await_bytes(kv.at[t, 0, pl.ds(0, SPAN - BLK)], x_recv.at[t, 0, 1])
        when(has_next, *[lambda n=n: forward_block(t, (x + n) % ROW).start() for n in (1, 3, 2)])

    def pass_back(h):
        await_bytes(qb.at[h, first_rows(h)], q_recv.at[h, 0])
        when(has_prev, lambda: backward(h).start())

    def await_first(h):
        for t in range(2):
            await_bytes(kv.at[t, h, first_rows(h)], x_recv.at[t, h, 0])

    def await_last(h):
        await_bytes(qb.at[h, last_rows(h)], q_recv.at[h, 1])

    for copy in id_copies:
        copy.wait()
    own_ids.wait()
    when(has_next, lambda: table_forward().start())
    when(has_prev, lambda: table_backward().start())

    def pair(query_slot, key_slot):
        d = query_slot - key_slot
        if d < 0 or d > WIN:
            return jnp.full((BLK, BLK), MASKED, jnp.float32)
        about = table[query_slot]
        column = jnp.transpose(about.astype(jnp.float32))
        there = table[key_slot].astype(jnp.float32)
        allowed = (there[0:1] == column[:, 0:1]) & (there[1:2] <= column[:, 1:2])
        if d:
            kind = about[1 + d:2 + d]
            if key_slot < ROW:
                kind = jnp.where(has_prev, kind, 0)
            allowed = (kind == 2) | ((kind == 1) & allowed)
        return jnp.where(allowed, 0.0, MASKED)

    def terms(ref, i, query_slot, slots):
        for n, slot in enumerate(slots):
            ref[i, :, n * BLK:(n + 1) * BLK] = pair(query_slot, slot)

    def score(queries, keys, term):
        return lax.dot_general(
            queries, keys, (((1,), (1,)), ((), ())), preferred_element_type=jnp.float32) + term

    def weigh(scores):
        highest = jnp.max(scores, axis=1, keepdims=True)
        weights = jnp.exp2((scores - highest) * FACTOR)
        return highest, jnp.sum(weights, axis=1, keepdims=True), weights.astype(jnp.bfloat16)

    def blend(weights, values):
        return jnp.dot(weights, values, preferred_element_type=jnp.float32)

    def block(i):
        return pl.ds(i * BLK if isinstance(i, int) else pl.multiple_of(i * BLK, BLK), BLK)

    def window(h, i):
        if isinstance(i, int) and i < BACK[h]:
            return pl.ds(BACK[h] * BLK, (ROW + 1 + i - BACK[h]) * BLK)
        return pl.ds(block(i).start, WINDOW)

    def partial(h):
        def rows(i):
            return pl.ds(SPAN + i * BLK, (BACK[h] - i) * BLK)

        def scores(i):
            return score(qn[h, block(i)], kv[0, h, rows(i)], bias_n[i, :, i * BLK:BACK[h] * BLK])

        following = scores(BACK[h] - 1)
        for i in reversed(range(BACK[h])):
            current = following
            if i:
                following = scores(i - 1)
            highest, total, weights = weigh(current)
            on[h, block(i)] = blend(weights, kv[1, h, rows(i)]).astype(jnp.bfloat16)
            lane = lax.broadcasted_iota(jnp.int32, (BLK, HD), 1)
            sn[h, i] = jnp.transpose(jnp.where(lane == 0, highest, total))[0:8]
            partial_out(h, i).start()
            partial_stats(h, i).start()

    def give_back(h, i):
        columns = pl.ds(pl.multiple_of(HD * (HEADS * me + h), HD), HD)
        for place in (2 * i, 2 * i + 1):
            rows = ob.at[h, pl.ds(pl.multiple_of(SHARE * place, SHARE), SHARE)]

            @pl.when(me != place)
            def _():
                remote(rows, o_ref.at[:, columns], o_send.at[h], o_recv.at[h], device(place)).start()

            @pl.when(me == place)
            def _():
                pltpu.make_async_copy(rows, o_ref.at[:, columns], o_recv.at[h]).start()

    def weigh_all(h):
        def scores(i):
            first = (BACK[h] - i) * BLK if i < BACK[h] else 0
            return score(qb[h, block(i)], kv[0, h, window(h, i)], bias[i, :, first:])

        following = scores(0)
        for i in range(ROW):
            current = following
            if i + 1 < ROW:
                following = scores(i + 1)
            tops[i], totals[i], weights_of[i, :, 0:window(h, i).size] = weigh(current)

    def blend_all(h):
        for i in range(ROW):
            rows = window(h, i)
            outs[i] = blend(weights_of[i, :, 0:rows.size], kv[1, h, rows])

    def merge(h):
        def body(n, carry):
            i = (x + 1 + n) % ROW

            @pl.when(has_prev & (i < BACK[h]))
            def _():
                partial_out(h, i).wait_recv()
                partial_stats(h, i).wait_recv()

            stats = jnp.transpose(sp[h, i])
            highest, other = tops[i], stats[:, 0:1]
            top = jnp.maximum(highest, other)
            here, there = jnp.exp2((highest - top) * FACTOR), jnp.exp2((other - top) * FACTOR)
            total = totals[i] * here + stats[:, 1:2] * there
            out = outs[i] * here + op[h, block(i)].astype(jnp.float32) * there
            ob[h, block(i)] = (out / total).astype(jnp.bfloat16)
            give_back(h, i)
            return carry

        lax.fori_loop(0, ROW, body, 0)

    def attend(*distances):
        def scores(chips):
            i = (x + ROW - chips) % ROW
            await_bytes(qb.at[0, block(i)], chip_recv.at[chips])
            return i, score(qb[0, block(i)], kv[0, 0, window(0, i)], bias[i])

        following = scores(distances[0])
        for n in range(len(distances)):
            i, current = following
            if n + 1 < len(distances):
                following = scores(distances[n + 1])
            _, total, weights = weigh(current)
            out = blend(weights, kv[1, 0, window(0, i)])
            ob[0, block(i)] = (out / total).astype(jnp.bfloat16)
            give_back(0, i)

    def await_keys(h):
        when(has_prev, lambda: forward(0, h).wait_recv())

    def await_values(h):
        when(has_prev, lambda: forward(1, h).wait_recv())

    def next_part(h):
        @pl.when(has_next)
        def _():
            backward(h).wait_recv()
            partial(h)

    pass_own(0)
    pass_own(1)
    pass_rest(0)
    when(has_prev, lambda: table_forward().wait_recv())
    for i in range(ROW):
        terms(bias, i, ROW + i, range(i, ROW + i + 1))

    @pl.when(has_next)
    def _():
        table_backward().wait_recv()
        for i in range(MOST):
            terms(bias_n, i, 2 * ROW + i, range(ROW, ROW + MOST))

    pass_rest(1)
    pass_back(1)
    pass_on(0, 1)
    pass_on(1, 1)
    await_first(1)
    next_part(1)
    pass_back(2)
    pass_on(0, 2)
    await_last(1)
    await_keys(1)
    weigh_all(1)
    pass_on(1, 2)
    await_values(1)
    blend_all(1)
    await_keys(0)
    await_values(0)
    attend(0)
    await_first(2)
    next_part(2)
    merge(1)
    await_last(2)
    await_keys(2)
    weigh_all(2)
    attend(1, 3, 2)
    await_values(2)
    blend_all(2)
    merge(2)

    sent = (TEAM - 1) * SHARE
    for h in range(HEADS):
        for t in range(2):
            await_bytes(kv.at[t, h, pl.ds(0, sent)], x_send.at[t, h])
        await_bytes(qb.at[h, pl.ds(0, sent)], q_send.at[h])

    @pl.when(has_next)
    def _():
        table_forward().wait_send()
        for h in range(HEADS):
            forward(0, h).wait_send()
            forward(1, h).wait_send()
        for h in SPLIT:
            for i in range(BACK[h]):
                partial_out(h, i).wait_send()
                partial_stats(h, i).wait_send()

    @pl.when(has_prev)
    def _():
        table_backward().wait_send()
        for h in SPLIT:
            backward(h).wait_send()

    for h in range(HEADS):
        await_bytes(qb.at[h, pl.ds(0, sent)], o_send.at[h])
        await_bytes(qb.at[h], o_recv.at[h])


def shards(queries, keys, values, clip_ids, group_ids, pair_kinds):
    hbm = pl.BlockSpec(memory_space=pl.ANY)
    vmem = pl.BlockSpec(memory_space=pltpu.VMEM)
    dma = pltpu.SemaphoreType.DMA
    bf16 = jnp.bfloat16
    return pl.pallas_call(
        kernel,
        out_shape=jax.ShapeDtypeStruct(queries.shape, bf16),
        in_specs=[hbm, hbm, hbm, vmem, vmem, pl.BlockSpec(memory_space=pltpu.SMEM)],
        out_specs=hbm,
        scratch_shapes=[
            pltpu.VMEM((8, BLK), jnp.int32),
            pltpu.VMEM((3 * ROW, 8, BLK), jnp.int32),
            pltpu.VMEM((2, HEADS, 2 * SPAN, HD), bf16),
            pltpu.VMEM((HEADS, SPAN, HD), bf16),
            pltpu.VMEM((HEADS, SPAN, HD), bf16),
            pltpu.VMEM((HEADS, MOST * BLK, HD), bf16),
            pltpu.VMEM((HEADS, MOST * BLK, HD), bf16),
            pltpu.VMEM((HEADS, MOST, 8, BLK), jnp.float32),
            pltpu.VMEM((HEADS, SPAN, HD), bf16),
            pltpu.VMEM((HEADS, ROW, 8, BLK), jnp.float32),
            pltpu.VMEM((ROW, BLK, WINDOW), jnp.float32),
            pltpu.VMEM((MOST, BLK, MOST * BLK), jnp.float32),
            pltpu.VMEM((ROW, BLK, 1), jnp.float32),
            pltpu.VMEM((ROW, BLK, 1), jnp.float32),
            pltpu.VMEM((ROW, BLK, HD), jnp.float32),
            pltpu.VMEM((ROW, BLK, WINDOW), bf16),
            dma((3,)), dma((4,)), dma, dma, dma, dma,
            dma((2, HEADS)), dma((2, HEADS, 2)), dma((HEADS,)), dma((HEADS, 2)),
            dma((2, HEADS)), dma((2, HEADS)), dma((ROW,)), dma((HEADS,)), dma((HEADS,)),
            dma((HEADS, MOST)), dma((HEADS, MOST)), dma((HEADS, MOST)), dma((HEADS, MOST)), dma((HEADS,)), dma((HEADS,)),
        ],
        compiler_params=pltpu.CompilerParams(
            collective_id=0, has_side_effects=True, vmem_limit_bytes=53 * 1024 * 1024),
    )(queries, keys, values, clip_ids.reshape(1, BLK), group_ids.reshape(1, BLK), pair_kinds)


def solution(mesh):
    tokens = P(("ctx", "head"), None)
    return jax.shard_map(
        shards, mesh=mesh, in_specs=(tokens, tokens, tokens, P("ctx"), P("ctx"), P("ctx", None)),
        out_specs=tokens, check_vma=False)
```

```python
import jax
import jax.numpy as jnp
from jax import lax
from jax.experimental import pallas as pl
from jax.experimental.pallas import tpu as pltpu
from jax.sharding import PartitionSpec as P

HD = 128
WIN = 4
BLK = 256
SHARE = 128
ROW = 4
TEAM = 2 * ROW
HEADS = 3
SPAN = ROW * BLK
WINDOW = (WIN + 1) * BLK
BACK = (0, 3, 3)
MOST = max(BACK)
SPLIT = tuple(h for h in range(HEADS) if BACK[h])
FIRST = (1, 0)
MESH = pl.DeviceIdType.MESH
FACTOR = 1.4426950408889634 * HD ** -0.5
MASKED = -1e30


def kernel(q_ref, k_ref, v_ref, clip_ref, group_ref, kinds_ref, o_ref,
           mine, table, kv, qb, ob, qn, on, sn, op, sp, bias, bias_n,
           tops, totals, outs, weights_of,
           id_send, id_recv, idf_send, idf_recv, idb_send, idb_recv, x_send, x_recv, q_send, q_recv, y_send, y_recv,
           chip_recv, qb_send, qb_recv, p_send, p_recv, s_send, s_recv, o_send, o_recv):
    ctx = lax.axis_index("ctx")
    core = lax.axis_index("head")
    x = ctx % ROW
    me = 2 * x + core
    base = ctx - x
    has_next = ctx < 128 - ROW
    has_prev = ctx >= ROW

    def device(place):
        return (base + place // 2, place % 2)

    after, before = (ctx + ROW, core), (ctx - ROW, core)

    def place_on(chips, c):
        return 2 * ((x + chips) % ROW) + c

    sibling = 2 * x + 1 - core
    partners = [place_on(chips, c) for c in (0, 1) for chips in (1, 2, 3)] + [sibling]

    barrier = pltpu.get_barrier_semaphore()
    for place in partners:
        pl.semaphore_signal(barrier, inc=1, device_id=device(place), device_id_type=MESH)

    @pl.when(has_next)
    def _():
        pl.semaphore_signal(barrier, inc=1, device_id=after, device_id_type=MESH)

    @pl.when(has_prev)
    def _():
        pl.semaphore_signal(barrier, inc=1, device_id=before, device_id_type=MESH)

    mine[0:1] = clip_ref[...]
    mine[1:2] = group_ref[...]
    for d in range(WIN):
        mine[2 + d:3 + d] = jnp.full((1, BLK), kinds_ref[0, d], jnp.int32)
    mine[6:8] = jnp.zeros((2, BLK), jnp.int32)

    for h in SPLIT:
        op[h, BACK[h] * BLK:] = jnp.zeros((SPAN - BACK[h] * BLK, HD), jnp.bfloat16)
        sp[h, BACK[h]:] = jnp.full((ROW - BACK[h], 8, BLK), MASKED, jnp.float32)

    @pl.when(jnp.logical_not(has_prev))
    def _():
        kv[:, :, 0:SPAN, :] = jnp.zeros((2, HEADS, SPAN, HD), jnp.bfloat16)
        table[0:ROW] = jnp.zeros((ROW, 8, BLK), jnp.int32)
        for h in SPLIT:
            op[h, 0:BACK[h] * BLK] = jnp.zeros((BACK[h] * BLK, HD), jnp.bfloat16)
            sp[h, 0:BACK[h]] = jnp.full((BACK[h], 8, BLK), MASKED, jnp.float32)

    pl.semaphore_wait(barrier, TEAM - 1 + jnp.where(has_next, 1, 0) + jnp.where(has_prev, 1, 0))

    id_copies = []
    for n, step in enumerate((2, 6, 4)):
        id_copies.append(pltpu.make_async_remote_copy(
            mine, table.at[ROW + x], id_send.at[n], id_recv.at[n],
            device_id=device((me + step) % TEAM), device_id_type=MESH))
        id_copies[-1].start()
    own_ids = pltpu.make_async_copy(mine, table.at[ROW + x], id_recv.at[3])
    own_ids.start()

    def remote(src, dst, send, recv, to):
        return pltpu.make_async_remote_copy(src, dst, send, recv, device_id=to, device_id_type=MESH)

    def share(ref, h, landing, send, recv, places):
        rows = pl.ds(pl.multiple_of(SHARE * me, SHARE), SHARE)
        for place in places:
            source = ref.at[:, pl.ds(pl.multiple_of(HD * (HEADS * place + h), HD), HD)]
            if place is me:
                pltpu.make_async_copy(source, landing.at[rows], recv).start()
            else:
                remote(source, landing.at[rows], send, recv, device(place)).start()

    own = pl.ds(SPAN, SPAN)
    here = (sibling, me)
    away = [place_on(chips, c) for c in FIRST for chips in (1, 3, 2)]
    everywhere = [*away, *here]

    def share_key(h, part, steps=everywhere):
        share(k_ref, h, kv.at[0, h, own], x_send.at[0, h], x_recv.at[0, h, part], steps)

    def share_value(h, part, steps=everywhere):
        share(v_ref, h, kv.at[1, h, own], x_send.at[1, h], x_recv.at[1, h, part], steps)

    def share_query(h, part):
        share(q_ref, h, qb.at[h], q_send.at[h], q_recv.at[h, part], everywhere)

    share_key(0, 0, here)
    share_value(0, 0, here)
    share_key(0, 1, away)
    share_value(0, 1, away)
    share(q_ref, 0, qb.at[0], q_send.at[0], chip_recv.at[0], here)
    for h in SPLIT:
        @pl.when(x < BACK[h])
        def _():
            share_query(h, 0)
            share_key(h, 0)
            share_value(h, 0)

        @pl.when(x >= BACK[h])
        def _():
            share_key(h, 1)
            share_value(h, 1)
            share_query(h, 1)

    for chips in (1, 3, 2):
        share(q_ref, 0, qb.at[0], q_send.at[0], chip_recv.at[chips], [place_on(chips, c) for c in FIRST])

    def await_bytes(ref, sem):
        pltpu.make_async_copy(ref, ref, sem).wait()

    def forward(t, h):
        first = BACK[h] * BLK
        return remote(kv.at[t, h, pl.ds(SPAN + first, SPAN - first)], kv.at[t, h, pl.ds(first, SPAN - first)],
                      y_send.at[t, h], y_recv.at[t, h], after)

    def forward_block(t, i):
        rows = pl.ds(pl.multiple_of(i * BLK, BLK), BLK)
        return remote(kv.at[t, 0, own].at[rows], kv.at[t, 0, rows], y_send.at[t, 0], y_recv.at[t, 0], after)

    def backward(h):
        first = pl.ds(0, BACK[h] * BLK)
        return remote(qb.at[h, first], qn.at[h, first], qb_send.at[h], qb_recv.at[h], before)

    def partial_out(h, i):
        return remote(on.at[h, pl.ds(i * BLK, BLK)], op.at[h, pl.ds(i * BLK, BLK)],
                      p_send.at[h, i], p_recv.at[h, i], after)

    def partial_stats(h, i):
        return remote(sn.at[h, i], sp.at[h, i], s_send.at[h, i], s_recv.at[h, i], after)

    def table_forward():
        return remote(table.at[pl.ds(ROW, ROW)], table.at[pl.ds(0, ROW)], idf_send, idf_recv, after)

    def table_backward():
        return remote(table.at[pl.ds(ROW, ROW)], table.at[pl.ds(2 * ROW, ROW)], idb_send, idb_recv, before)

    def when(condition, *actions):
        @pl.when(condition)
        def _():
            for action in actions:
                action()

    def first_rows(h):
        return pl.ds(0, BACK[h] * BLK)

    def last_rows(h):
        return pl.ds(BACK[h] * BLK, SPAN - BACK[h] * BLK)

    def pass_on(t, h):
        await_bytes(kv.at[t, h, last_rows(h)], x_recv.at[t, h, 1])
        when(has_next, lambda: forward(t, h).start())

    def pass_own(t):
        await_bytes(kv.at[t, 0, pl.ds(0, BLK)], x_recv.at[t, 0, 0])
        when(has_next, lambda: forward_block(t, x).start())

    def pass_rest(t):
        await_bytes(kv.at[t, 0, pl.ds(0, SPAN - BLK)], x_recv.at[t, 0, 1])
        when(has_next, *[lambda n=n: forward_block(t, (x + n) % ROW).start() for n in (1, 3, 2)])

    def pass_back(h):
        await_bytes(qb.at[h, first_rows(h)], q_recv.at[h, 0])
        when(has_prev, lambda: backward(h).start())

    def await_first(h):
        for t in range(2):
            await_bytes(kv.at[t, h, first_rows(h)], x_recv.at[t, h, 0])

    def await_last(h):
        await_bytes(qb.at[h, last_rows(h)], q_recv.at[h, 1])

    for copy in id_copies:
        copy.wait()
    own_ids.wait()
    when(has_next, lambda: table_forward().start())
    when(has_prev, lambda: table_backward().start())

    def pair(query_slot, key_slot):
        d = query_slot - key_slot
        if d < 0 or d > WIN:
            return jnp.full((BLK, BLK), MASKED, jnp.float32)
        about = table[query_slot]
        column = jnp.transpose(about.astype(jnp.float32))
        there = table[key_slot].astype(jnp.float32)
        allowed = (there[0:1] == column[:, 0:1]) & (there[1:2] <= column[:, 1:2])
        if d:
            kind = about[1 + d:2 + d]
            if key_slot < ROW:
                kind = jnp.where(has_prev, kind, 0)
            allowed = (kind == 2) | ((kind == 1) & allowed)
        return jnp.where(allowed, 0.0, MASKED)

    def terms(ref, i, query_slot, slots):
        for n, slot in enumerate(slots):
            ref[i, :, n * BLK:(n + 1) * BLK] = pair(query_slot, slot)

    def score(queries, keys, term):
        return lax.dot_general(
            queries, keys, (((1,), (1,)), ((), ())), preferred_element_type=jnp.float32) + term

    def weigh(scores):
        highest = jnp.max(scores, axis=1, keepdims=True)
        weights = jnp.exp2((scores - highest) * FACTOR)
        return highest, jnp.sum(weights, axis=1, keepdims=True), weights.astype(jnp.bfloat16)

    def blend(weights, values):
        return jnp.dot(weights, values, preferred_element_type=jnp.float32)

    def block(i):
        return pl.ds(i * BLK if isinstance(i, int) else pl.multiple_of(i * BLK, BLK), BLK)

    def window(h, i):
        if isinstance(i, int) and i < BACK[h]:
            return pl.ds(BACK[h] * BLK, (ROW + 1 + i - BACK[h]) * BLK)
        return pl.ds(block(i).start, WINDOW)

    def partial(h):
        def rows(i):
            return pl.ds(SPAN + i * BLK, (BACK[h] - i) * BLK)

        def scores(i):
            return score(qn[h, block(i)], kv[0, h, rows(i)], bias_n[i, :, i * BLK:BACK[h] * BLK])

        following = scores(BACK[h] - 1)
        for i in reversed(range(BACK[h])):
            current = following
            if i:
                following = scores(i - 1)
            highest, total, weights = weigh(current)
            on[h, block(i)] = blend(weights, kv[1, h, rows(i)]).astype(jnp.bfloat16)
            lane = lax.broadcasted_iota(jnp.int32, (BLK, HD), 1)
            sn[h, i] = jnp.transpose(jnp.where(lane == 0, highest, total))[0:8]
            partial_out(h, i).start()
            partial_stats(h, i).start()

    def give_back(h, i):
        columns = pl.ds(pl.multiple_of(HD * (HEADS * me + h), HD), HD)
        for place in (2 * i + 1, 2 * i):
            rows = ob.at[h, pl.ds(pl.multiple_of(SHARE * place, SHARE), SHARE)]

            @pl.when(me != place)
            def _():
                remote(rows, o_ref.at[:, columns], o_send.at[h], o_recv.at[h], device(place)).start()

            @pl.when(me == place)
            def _():
                pltpu.make_async_copy(rows, o_ref.at[:, columns], o_recv.at[h]).start()

    def weigh_all(h):
        def scores(i):
            first = (BACK[h] - i) * BLK if i < BACK[h] else 0
            return score(qb[h, block(i)], kv[0, h, window(h, i)], bias[i, :, first:])

        following = scores(0)
        for i in range(ROW):
            current = following
            if i + 1 < ROW:
                following = scores(i + 1)
            tops[i], totals[i], weights_of[i, :, 0:window(h, i).size] = weigh(current)

    def blend_all(h):
        for i in range(ROW):
            rows = window(h, i)
            outs[i] = blend(weights_of[i, :, 0:rows.size], kv[1, h, rows])

    def merge(h):
        def body(n, carry):
            i = (x + 1 + n) % ROW

            @pl.when(has_prev & (i < BACK[h]))
            def _():
                partial_out(h, i).wait_recv()
                partial_stats(h, i).wait_recv()

            stats = jnp.transpose(sp[h, i])
            highest, other = tops[i], stats[:, 0:1]
            top = jnp.maximum(highest, other)
            here, there = jnp.exp2((highest - top) * FACTOR), jnp.exp2((other - top) * FACTOR)
            total = totals[i] * here + stats[:, 1:2] * there
            out = outs[i] * here + op[h, block(i)].astype(jnp.float32) * there
            ob[h, block(i)] = (out / total).astype(jnp.bfloat16)
            give_back(h, i)
            return carry

        lax.fori_loop(0, ROW, body, 0)

    def attend(*distances):
        def scores(chips):
            i = (x + ROW - chips) % ROW
            await_bytes(qb.at[0, block(i)], chip_recv.at[chips])
            return i, score(qb[0, block(i)], kv[0, 0, window(0, i)], bias[i])

        following = scores(distances[0])
        for n in range(len(distances)):
            i, current = following
            if n + 1 < len(distances):
                following = scores(distances[n + 1])
            _, total, weights = weigh(current)
            out = blend(weights, kv[1, 0, window(0, i)])
            ob[0, block(i)] = (out / total).astype(jnp.bfloat16)
            give_back(0, i)

    def await_keys(h):
        when(has_prev, lambda: forward(0, h).wait_recv())

    def await_values(h):
        when(has_prev, lambda: forward(1, h).wait_recv())

    def next_part(h):
        @pl.when(has_next)
        def _():
            backward(h).wait_recv()
            partial(h)

    pass_own(0)
    pass_own(1)
    pass_rest(0)
    when(has_prev, lambda: table_forward().wait_recv())
    for i in range(ROW):
        terms(bias, i, ROW + i, range(i, ROW + i + 1))

    @pl.when(has_next)
    def _():
        table_backward().wait_recv()
        for i in range(MOST):
            terms(bias_n, i, 2 * ROW + i, range(ROW, ROW + MOST))

    pass_rest(1)
    pass_back(1)
    pass_on(0, 1)
    pass_on(1, 1)
    await_first(1)
    next_part(1)
    pass_back(2)
    pass_on(0, 2)
    await_last(1)
    await_keys(1)
    weigh_all(1)
    pass_on(1, 2)
    await_values(1)
    blend_all(1)
    await_keys(0)
    await_values(0)
    await_first(2)
    next_part(2)
    merge(1)
    attend(1, 3, 2)
    await_last(2)
    await_keys(2)
    weigh_all(2)
    await_values(2)
    blend_all(2)
    merge(2)
    attend(0)

    sent = (TEAM - 1) * SHARE
    for h in range(HEADS):
        for t in range(2):
            await_bytes(kv.at[t, h, pl.ds(0, sent)], x_send.at[t, h])
        await_bytes(qb.at[h, pl.ds(0, sent)], q_send.at[h])

    @pl.when(has_next)
    def _():
        table_forward().wait_send()
        for h in range(HEADS):
            forward(0, h).wait_send()
            forward(1, h).wait_send()
        for h in SPLIT:
            for i in range(BACK[h]):
                partial_out(h, i).wait_send()
                partial_stats(h, i).wait_send()

    @pl.when(has_prev)
    def _():
        table_backward().wait_send()
        for h in SPLIT:
            backward(h).wait_send()

    for h in range(HEADS):
        await_bytes(qb.at[h, pl.ds(0, sent)], o_send.at[h])
        await_bytes(qb.at[h], o_recv.at[h])


def shards(queries, keys, values, clip_ids, group_ids, pair_kinds):
    hbm = pl.BlockSpec(memory_space=pl.ANY)
    vmem = pl.BlockSpec(memory_space=pltpu.VMEM)
    dma = pltpu.SemaphoreType.DMA
    bf16 = jnp.bfloat16
    return pl.pallas_call(
        kernel,
        out_shape=jax.ShapeDtypeStruct(queries.shape, bf16),
        in_specs=[hbm, hbm, hbm, vmem, vmem, pl.BlockSpec(memory_space=pltpu.SMEM)],
        out_specs=hbm,
        scratch_shapes=[
            pltpu.VMEM((8, BLK), jnp.int32),
            pltpu.VMEM((3 * ROW, 8, BLK), jnp.int32),
            pltpu.VMEM((2, HEADS, 2 * SPAN, HD), bf16),
            pltpu.VMEM((HEADS, SPAN, HD), bf16),
            pltpu.VMEM((HEADS, SPAN, HD), bf16),
            pltpu.VMEM((HEADS, MOST * BLK, HD), bf16),
            pltpu.VMEM((HEADS, MOST * BLK, HD), bf16),
            pltpu.VMEM((HEADS, MOST, 8, BLK), jnp.float32),
            pltpu.VMEM((HEADS, SPAN, HD), bf16),
            pltpu.VMEM((HEADS, ROW, 8, BLK), jnp.float32),
            pltpu.VMEM((ROW, BLK, WINDOW), jnp.float32),
            pltpu.VMEM((MOST, BLK, MOST * BLK), jnp.float32),
            pltpu.VMEM((ROW, BLK, 1), jnp.float32),
            pltpu.VMEM((ROW, BLK, 1), jnp.float32),
            pltpu.VMEM((ROW, BLK, HD), jnp.float32),
            pltpu.VMEM((ROW, BLK, WINDOW), bf16),
            dma((3,)), dma((4,)), dma, dma, dma, dma,
            dma((2, HEADS)), dma((2, HEADS, 2)), dma((HEADS,)), dma((HEADS, 2)),
            dma((2, HEADS)), dma((2, HEADS)), dma((ROW,)), dma((HEADS,)), dma((HEADS,)),
            dma((HEADS, MOST)), dma((HEADS, MOST)), dma((HEADS, MOST)), dma((HEADS, MOST)), dma((HEADS,)), dma((HEADS,)),
        ],
        compiler_params=pltpu.CompilerParams(
            collective_id=0, has_side_effects=True, vmem_limit_bytes=53 * 1024 * 1024),
    )(queries, keys, values, clip_ids.reshape(1, BLK), group_ids.reshape(1, BLK), pair_kinds)


def solution(mesh):
    tokens = P(("ctx", "head"), None)
    return jax.shard_map(
        shards, mesh=mesh, in_specs=(tokens, tokens, tokens, P("ctx"), P("ctx"), P("ctx", None)),
        out_specs=tokens, check_vma=False)
```

```python
import jax
import jax.numpy as jnp
from jax import lax
from jax.experimental import pallas as pl
from jax.experimental.pallas import tpu as pltpu
from jax.sharding import PartitionSpec as P

HD = 128
WIN = 4
BLK = 256
SHARE = 128
ROW = 4
TEAM = 2 * ROW
HEADS = 3
SPAN = ROW * BLK
WINDOW = (WIN + 1) * BLK
BACK = (0, 3, 3)
MOST = max(BACK)
SPLIT = tuple(h for h in range(HEADS) if BACK[h])
FIRST = (1, 0)
MESH = pl.DeviceIdType.MESH
FACTOR = 1.4426950408889634 * HD ** -0.5
MASKED = -1e30


def kernel(q_ref, k_ref, v_ref, clip_ref, group_ref, kinds_ref, o_ref,
           mine, table, kv, qb, ob, qn, on, sn, op, sp, bias, bias_n,
           tops, totals, outs, weights_of,
           id_send, id_recv, idf_send, idf_recv, idb_send, idb_recv, x_send, x_recv, q_send, q_recv, y_send, y_recv,
           chip_recv, qb_send, qb_recv, p_send, p_recv, s_send, s_recv, o_send, o_recv):
    ctx = lax.axis_index("ctx")
    core = lax.axis_index("head")
    x = ctx % ROW
    me = 2 * x + core
    base = ctx - x
    has_next = ctx < 128 - ROW
    has_prev = ctx >= ROW

    def device(place):
        return (base + place // 2, place % 2)

    after, before = (ctx + ROW, core), (ctx - ROW, core)

    def place_on(chips, c):
        return 2 * ((x + chips) % ROW) + c

    sibling = 2 * x + 1 - core
    partners = [place_on(chips, c) for c in (0, 1) for chips in (1, 2, 3)] + [sibling]

    barrier = pltpu.get_barrier_semaphore()
    for place in partners:
        pl.semaphore_signal(barrier, inc=1, device_id=device(place), device_id_type=MESH)

    @pl.when(has_next)
    def _():
        pl.semaphore_signal(barrier, inc=1, device_id=after, device_id_type=MESH)

    @pl.when(has_prev)
    def _():
        pl.semaphore_signal(barrier, inc=1, device_id=before, device_id_type=MESH)

    mine[0:1] = clip_ref[...]
    mine[1:2] = group_ref[...]
    for d in range(WIN):
        mine[2 + d:3 + d] = jnp.full((1, BLK), kinds_ref[0, d], jnp.int32)
    mine[6:8] = jnp.zeros((2, BLK), jnp.int32)

    for h in SPLIT:
        op[h, BACK[h] * BLK:] = jnp.zeros((SPAN - BACK[h] * BLK, HD), jnp.bfloat16)
        sp[h, BACK[h]:] = jnp.full((ROW - BACK[h], 8, BLK), MASKED, jnp.float32)

    @pl.when(jnp.logical_not(has_prev))
    def _():
        kv[:, :, 0:SPAN, :] = jnp.zeros((2, HEADS, SPAN, HD), jnp.bfloat16)
        table[0:ROW] = jnp.zeros((ROW, 8, BLK), jnp.int32)
        for h in SPLIT:
            op[h, 0:BACK[h] * BLK] = jnp.zeros((BACK[h] * BLK, HD), jnp.bfloat16)
            sp[h, 0:BACK[h]] = jnp.full((BACK[h], 8, BLK), MASKED, jnp.float32)

    pl.semaphore_wait(barrier, TEAM - 1 + jnp.where(has_next, 1, 0) + jnp.where(has_prev, 1, 0))

    id_copies = []
    for n, step in enumerate((2, 6, 4)):
        id_copies.append(pltpu.make_async_remote_copy(
            mine, table.at[ROW + x], id_send.at[n], id_recv.at[n],
            device_id=device((me + step) % TEAM), device_id_type=MESH))
        id_copies[-1].start()
    own_ids = pltpu.make_async_copy(mine, table.at[ROW + x], id_recv.at[3])
    own_ids.start()

    def remote(src, dst, send, recv, to):
        return pltpu.make_async_remote_copy(src, dst, send, recv, device_id=to, device_id_type=MESH)

    def share(ref, h, landing, send, recv, places):
        rows = pl.ds(pl.multiple_of(SHARE * me, SHARE), SHARE)
        for place in places:
            source = ref.at[:, pl.ds(pl.multiple_of(HD * (HEADS * place + h), HD), HD)]
            if place is me:
                pltpu.make_async_copy(source, landing.at[rows], recv).start()
            else:
                remote(source, landing.at[rows], send, recv, device(place)).start()

    own = pl.ds(SPAN, SPAN)
    here = (sibling, me)
    away = [place_on(chips, c) for c in FIRST for chips in (2, 1, 3)]
    everywhere = [*away, *here]

    def share_key(h, part, steps=everywhere):
        share(k_ref, h, kv.at[0, h, own], x_send.at[0, h], x_recv.at[0, h, part], steps)

    def share_value(h, part, steps=everywhere):
        share(v_ref, h, kv.at[1, h, own], x_send.at[1, h], x_recv.at[1, h, part], steps)

    def share_query(h, part):
        share(q_ref, h, qb.at[h], q_send.at[h], q_recv.at[h, part], everywhere)

    share_key(0, 0, here)
    share_value(0, 0, here)
    share_key(0, 1, away)
    share_value(0, 1, away)
    share(q_ref, 0, qb.at[0], q_send.at[0], chip_recv.at[0], here)
    for h in SPLIT:
        @pl.when(x < BACK[h])
        def _():
            share_query(h, 0)
            share_key(h, 0)
            share_value(h, 0)

        @pl.when(x >= BACK[h])
        def _():
            share_key(h, 1)
            share_value(h, 1)
            share_query(h, 1)

    for chips in (1, 3, 2):
        share(q_ref, 0, qb.at[0], q_send.at[0], chip_recv.at[chips], [place_on(chips, c) for c in FIRST])

    def await_bytes(ref, sem):
        pltpu.make_async_copy(ref, ref, sem).wait()

    def forward(t, h):
        first = BACK[h] * BLK
        return remote(kv.at[t, h, pl.ds(SPAN + first, SPAN - first)], kv.at[t, h, pl.ds(first, SPAN - first)],
                      y_send.at[t, h], y_recv.at[t, h], after)

    def forward_block(t, i):
        rows = pl.ds(pl.multiple_of(i * BLK, BLK), BLK)
        return remote(kv.at[t, 0, own].at[rows], kv.at[t, 0, rows], y_send.at[t, 0], y_recv.at[t, 0], after)

    def backward(h):
        first = pl.ds(0, BACK[h] * BLK)
        return remote(qb.at[h, first], qn.at[h, first], qb_send.at[h], qb_recv.at[h], before)

    def partial_out(h, i):
        return remote(on.at[h, pl.ds(i * BLK, BLK)], op.at[h, pl.ds(i * BLK, BLK)],
                      p_send.at[h, i], p_recv.at[h, i], after)

    def partial_stats(h, i):
        return remote(sn.at[h, i], sp.at[h, i], s_send.at[h, i], s_recv.at[h, i], after)

    def table_forward():
        return remote(table.at[pl.ds(ROW, ROW)], table.at[pl.ds(0, ROW)], idf_send, idf_recv, after)

    def table_backward():
        return remote(table.at[pl.ds(ROW, ROW)], table.at[pl.ds(2 * ROW, ROW)], idb_send, idb_recv, before)

    def when(condition, *actions):
        @pl.when(condition)
        def _():
            for action in actions:
                action()

    def first_rows(h):
        return pl.ds(0, BACK[h] * BLK)

    def last_rows(h):
        return pl.ds(BACK[h] * BLK, SPAN - BACK[h] * BLK)

    def pass_on(t, h):
        await_bytes(kv.at[t, h, last_rows(h)], x_recv.at[t, h, 1])
        when(has_next, lambda: forward(t, h).start())

    def pass_own(t):
        await_bytes(kv.at[t, 0, pl.ds(0, BLK)], x_recv.at[t, 0, 0])
        when(has_next, lambda: forward_block(t, x).start())

    def pass_rest(t):
        await_bytes(kv.at[t, 0, pl.ds(0, SPAN - BLK)], x_recv.at[t, 0, 1])
        when(has_next, *[lambda n=n: forward_block(t, (x + n) % ROW).start() for n in (1, 3, 2)])

    def pass_back(h):
        await_bytes(qb.at[h, first_rows(h)], q_recv.at[h, 0])
        when(has_prev, lambda: backward(h).start())

    def await_first(h):
        for t in range(2):
            await_bytes(kv.at[t, h, first_rows(h)], x_recv.at[t, h, 0])

    def await_last(h):
        await_bytes(qb.at[h, last_rows(h)], q_recv.at[h, 1])

    for copy in id_copies:
        copy.wait()
    own_ids.wait()
    when(has_next, lambda: table_forward().start())
    when(has_prev, lambda: table_backward().start())

    def pair(query_slot, key_slot):
        d = query_slot - key_slot
        if d < 0 or d > WIN:
            return jnp.full((BLK, BLK), MASKED, jnp.float32)
        about = table[query_slot]
        column = jnp.transpose(about.astype(jnp.float32))
        there = table[key_slot].astype(jnp.float32)
        allowed = (there[0:1] == column[:, 0:1]) & (there[1:2] <= column[:, 1:2])
        if d:
            kind = about[1 + d:2 + d]
            if key_slot < ROW:
                kind = jnp.where(has_prev, kind, 0)
            allowed = (kind == 2) | ((kind == 1) & allowed)
        return jnp.where(allowed, 0.0, MASKED)

    def terms(ref, i, query_slot, slots):
        for n, slot in enumerate(slots):
            ref[i, :, n * BLK:(n + 1) * BLK] = pair(query_slot, slot)

    def score(queries, keys, term):
        return lax.dot_general(
            queries, keys, (((1,), (1,)), ((), ())), preferred_element_type=jnp.float32) + term

    def weigh(scores):
        highest = jnp.max(scores, axis=1, keepdims=True)
        weights = jnp.exp2((scores - highest) * FACTOR)
        return highest, jnp.sum(weights, axis=1, keepdims=True), weights.astype(jnp.bfloat16)

    def blend(weights, values):
        return jnp.dot(weights, values, preferred_element_type=jnp.float32)

    def block(i):
        return pl.ds(i * BLK if isinstance(i, int) else pl.multiple_of(i * BLK, BLK), BLK)

    def window(h, i):
        if isinstance(i, int) and i < BACK[h]:
            return pl.ds(BACK[h] * BLK, (ROW + 1 + i - BACK[h]) * BLK)
        return pl.ds(block(i).start, WINDOW)

    def partial(h):
        def rows(i):
            return pl.ds(SPAN + i * BLK, (BACK[h] - i) * BLK)

        def scores(i):
            return score(qn[h, block(i)], kv[0, h, rows(i)], bias_n[i, :, i * BLK:BACK[h] * BLK])

        following = scores(BACK[h] - 1)
        for i in reversed(range(BACK[h])):
            current = following
            if i:
                following = scores(i - 1)
            highest, total, weights = weigh(current)
            on[h, block(i)] = blend(weights, kv[1, h, rows(i)]).astype(jnp.bfloat16)
            lane = lax.broadcasted_iota(jnp.int32, (BLK, HD), 1)
            sn[h, i] = jnp.transpose(jnp.where(lane == 0, highest, total))[0:8]
            partial_out(h, i).start()
            partial_stats(h, i).start()

    def give_back(h, i):
        columns = pl.ds(pl.multiple_of(HD * (HEADS * me + h), HD), HD)
        for place in (2 * i + 1, 2 * i):
            rows = ob.at[h, pl.ds(pl.multiple_of(SHARE * place, SHARE), SHARE)]

            @pl.when(me != place)
            def _():
                remote(rows, o_ref.at[:, columns], o_send.at[h], o_recv.at[h], device(place)).start()

            @pl.when(me == place)
            def _():
                pltpu.make_async_copy(rows, o_ref.at[:, columns], o_recv.at[h]).start()

    def weigh_all(h):
        def scores(i):
            first = (BACK[h] - i) * BLK if i < BACK[h] else 0
            return score(qb[h, block(i)], kv[0, h, window(h, i)], bias[i, :, first:])

        following = scores(0)
        for i in range(ROW):
            current = following
            if i + 1 < ROW:
                following = scores(i + 1)
            tops[i], totals[i], weights_of[i, :, 0:window(h, i).size] = weigh(current)

    def blend_all(h):
        for i in range(ROW):
            rows = window(h, i)
            outs[i] = blend(weights_of[i, :, 0:rows.size], kv[1, h, rows])

    def merge(h):
        def body(n, carry):
            i = (x + 1 + n) % ROW

            @pl.when(has_prev & (i < BACK[h]))
            def _():
                partial_out(h, i).wait_recv()
                partial_stats(h, i).wait_recv()

            stats = jnp.transpose(sp[h, i])
            highest, other = tops[i], stats[:, 0:1]
            top = jnp.maximum(highest, other)
            here, there = jnp.exp2((highest - top) * FACTOR), jnp.exp2((other - top) * FACTOR)
            total = totals[i] * here + stats[:, 1:2] * there
            out = outs[i] * here + op[h, block(i)].astype(jnp.float32) * there
            ob[h, block(i)] = (out / total).astype(jnp.bfloat16)
            give_back(h, i)
            return carry

        lax.fori_loop(0, ROW, body, 0)

    def attend(*distances):
        def scores(chips):
            i = (x + ROW - chips) % ROW
            await_bytes(qb.at[0, block(i)], chip_recv.at[chips])
            return i, score(qb[0, block(i)], kv[0, 0, window(0, i)], bias[i])

        following = scores(distances[0])
        for n in range(len(distances)):
            i, current = following
            if n + 1 < len(distances):
                following = scores(distances[n + 1])
            _, total, weights = weigh(current)
            out = blend(weights, kv[1, 0, window(0, i)])
            ob[0, block(i)] = (out / total).astype(jnp.bfloat16)
            give_back(0, i)

    def await_keys(h):
        when(has_prev, lambda: forward(0, h).wait_recv())

    def await_values(h):
        when(has_prev, lambda: forward(1, h).wait_recv())

    def next_part(h):
        @pl.when(has_next)
        def _():
            backward(h).wait_recv()
            partial(h)

    pass_own(0)
    pass_own(1)
    pass_rest(0)
    when(has_prev, lambda: table_forward().wait_recv())
    for i in range(ROW):
        terms(bias, i, ROW + i, range(i, ROW + i + 1))

    @pl.when(has_next)
    def _():
        table_backward().wait_recv()
        for i in range(MOST):
            terms(bias_n, i, 2 * ROW + i, range(ROW, ROW + MOST))

    pass_rest(1)
    pass_back(1)
    pass_on(0, 1)
    pass_on(1, 1)
    await_first(1)
    next_part(1)
    pass_back(2)
    pass_on(0, 2)
    await_last(1)
    await_keys(1)
    weigh_all(1)
    pass_on(1, 2)
    await_values(1)
    blend_all(1)
    await_keys(0)
    await_values(0)
    await_first(2)
    next_part(2)
    merge(1)
    attend(1, 3, 2)
    await_last(2)
    await_keys(2)
    weigh_all(2)
    await_values(2)
    blend_all(2)
    merge(2)
    attend(0)

    sent = (TEAM - 1) * SHARE
    for h in range(HEADS):
        for t in range(2):
            await_bytes(kv.at[t, h, pl.ds(0, sent)], x_send.at[t, h])
        await_bytes(qb.at[h, pl.ds(0, sent)], q_send.at[h])

    @pl.when(has_next)
    def _():
        table_forward().wait_send()
        for h in range(HEADS):
            forward(0, h).wait_send()
            forward(1, h).wait_send()
        for h in SPLIT:
            for i in range(BACK[h]):
                partial_out(h, i).wait_send()
                partial_stats(h, i).wait_send()

    @pl.when(has_prev)
    def _():
        table_backward().wait_send()
        for h in SPLIT:
            backward(h).wait_send()

    for h in range(HEADS):
        await_bytes(qb.at[h, pl.ds(0, sent)], o_send.at[h])
        await_bytes(qb.at[h], o_recv.at[h])


def shards(queries, keys, values, clip_ids, group_ids, pair_kinds):
    hbm = pl.BlockSpec(memory_space=pl.ANY)
    vmem = pl.BlockSpec(memory_space=pltpu.VMEM)
    dma = pltpu.SemaphoreType.DMA
    bf16 = jnp.bfloat16
    return pl.pallas_call(
        kernel,
        out_shape=jax.ShapeDtypeStruct(queries.shape, bf16),
        in_specs=[hbm, hbm, hbm, vmem, vmem, pl.BlockSpec(memory_space=pltpu.SMEM)],
        out_specs=hbm,
        scratch_shapes=[
            pltpu.VMEM((8, BLK), jnp.int32),
            pltpu.VMEM((3 * ROW, 8, BLK), jnp.int32),
            pltpu.VMEM((2, HEADS, 2 * SPAN, HD), bf16),
            pltpu.VMEM((HEADS, SPAN, HD), bf16),
            pltpu.VMEM((HEADS, SPAN, HD), bf16),
            pltpu.VMEM((HEADS, MOST * BLK, HD), bf16),
            pltpu.VMEM((HEADS, MOST * BLK, HD), bf16),
            pltpu.VMEM((HEADS, MOST, 8, BLK), jnp.float32),
            pltpu.VMEM((HEADS, SPAN, HD), bf16),
            pltpu.VMEM((HEADS, ROW, 8, BLK), jnp.float32),
            pltpu.VMEM((ROW, BLK, WINDOW), jnp.float32),
            pltpu.VMEM((MOST, BLK, MOST * BLK), jnp.float32),
            pltpu.VMEM((ROW, BLK, 1), jnp.float32),
            pltpu.VMEM((ROW, BLK, 1), jnp.float32),
            pltpu.VMEM((ROW, BLK, HD), jnp.float32),
            pltpu.VMEM((ROW, BLK, WINDOW), bf16),
            dma((3,)), dma((4,)), dma, dma, dma, dma,
            dma((2, HEADS)), dma((2, HEADS, 2)), dma((HEADS,)), dma((HEADS, 2)),
            dma((2, HEADS)), dma((2, HEADS)), dma((ROW,)), dma((HEADS,)), dma((HEADS,)),
            dma((HEADS, MOST)), dma((HEADS, MOST)), dma((HEADS, MOST)), dma((HEADS, MOST)), dma((HEADS,)), dma((HEADS,)),
        ],
        compiler_params=pltpu.CompilerParams(
            collective_id=0, has_side_effects=True, vmem_limit_bytes=53 * 1024 * 1024),
    )(queries, keys, values, clip_ids.reshape(1, BLK), group_ids.reshape(1, BLK), pair_kinds)


def solution(mesh):
    tokens = P(("ctx", "head"), None)
    return jax.shard_map(
        shards, mesh=mesh, in_specs=(tokens, tokens, tokens, P("ctx"), P("ctx"), P("ctx", None)),
        out_specs=tokens, check_vma=False)
```

```python
import jax
import jax.numpy as jnp
from jax import lax
from jax.experimental import pallas as pl
from jax.experimental.pallas import tpu as pltpu
from jax.sharding import PartitionSpec as P

HD = 128
WIN = 4
BLK = 256
SHARE = 128
ROW = 4
TEAM = 2 * ROW
HEADS = 3
SPAN = ROW * BLK
WINDOW = (WIN + 1) * BLK
BACK = (0, 3, 3)
MOST = max(BACK)
SPLIT = tuple(h for h in range(HEADS) if BACK[h])
FIRST = (1, 0)
MESH = pl.DeviceIdType.MESH
FACTOR = 1.4426950408889634 * HD ** -0.5
MASKED = -1e30


def kernel(q_ref, k_ref, v_ref, clip_ref, group_ref, kinds_ref, o_ref,
           mine, table, kv, qb, ob, qn, on, sn, op, sp, bias, bias_n,
           tops, totals, outs, weights_of,
           id_send, id_recv, idf_send, idf_recv, idb_send, idb_recv, x_send, x_recv, q_send, q_recv, y_send, y_recv,
           chip_recv, qb_send, qb_recv, p_send, p_recv, s_send, s_recv, o_send, o_recv):
    ctx = lax.axis_index("ctx")
    core = lax.axis_index("head")
    x = ctx % ROW
    me = 2 * x + core
    base = ctx - x
    has_next = ctx < 128 - ROW
    has_prev = ctx >= ROW

    def device(place):
        return (base + place // 2, place % 2)

    after, before = (ctx + ROW, core), (ctx - ROW, core)

    def place_on(chips, c):
        return 2 * ((x + chips) % ROW) + c

    sibling = 2 * x + 1 - core
    partners = [place_on(chips, c) for c in (0, 1) for chips in (1, 2, 3)] + [sibling]

    barrier = pltpu.get_barrier_semaphore()
    for place in partners:
        pl.semaphore_signal(barrier, inc=1, device_id=device(place), device_id_type=MESH)

    @pl.when(has_next)
    def _():
        pl.semaphore_signal(barrier, inc=1, device_id=after, device_id_type=MESH)

    @pl.when(has_prev)
    def _():
        pl.semaphore_signal(barrier, inc=1, device_id=before, device_id_type=MESH)

    mine[0:1] = clip_ref[...]
    mine[1:2] = group_ref[...]
    for d in range(WIN):
        mine[2 + d:3 + d] = jnp.full((1, BLK), kinds_ref[0, d], jnp.int32)
    mine[6:8] = jnp.zeros((2, BLK), jnp.int32)

    for h in SPLIT:
        op[h, BACK[h] * BLK:] = jnp.zeros((SPAN - BACK[h] * BLK, HD), jnp.bfloat16)
        sp[h, BACK[h]:] = jnp.full((ROW - BACK[h], 8, BLK), MASKED, jnp.float32)

    @pl.when(jnp.logical_not(has_prev))
    def _():
        kv[:, :, 0:SPAN, :] = jnp.zeros((2, HEADS, SPAN, HD), jnp.bfloat16)
        table[0:ROW] = jnp.zeros((ROW, 8, BLK), jnp.int32)
        for h in SPLIT:
            op[h, 0:BACK[h] * BLK] = jnp.zeros((BACK[h] * BLK, HD), jnp.bfloat16)
            sp[h, 0:BACK[h]] = jnp.full((BACK[h], 8, BLK), MASKED, jnp.float32)

    pl.semaphore_wait(barrier, TEAM - 1 + jnp.where(has_next, 1, 0) + jnp.where(has_prev, 1, 0))

    id_copies = []
    for n, step in enumerate((2, 6, 4)):
        id_copies.append(pltpu.make_async_remote_copy(
            mine, table.at[ROW + x], id_send.at[n], id_recv.at[n],
            device_id=device((me + step) % TEAM), device_id_type=MESH))
        id_copies[-1].start()
    own_ids = pltpu.make_async_copy(mine, table.at[ROW + x], id_recv.at[3])
    own_ids.start()

    def remote(src, dst, send, recv, to):
        return pltpu.make_async_remote_copy(src, dst, send, recv, device_id=to, device_id_type=MESH)

    def share(ref, h, landing, send, recv, places):
        rows = pl.ds(pl.multiple_of(SHARE * me, SHARE), SHARE)
        for place in places:
            source = ref.at[:, pl.ds(pl.multiple_of(HD * (HEADS * place + h), HD), HD)]
            if place is me:
                pltpu.make_async_copy(source, landing.at[rows], recv).start()
            else:
                remote(source, landing.at[rows], send, recv, device(place)).start()

    own = pl.ds(SPAN, SPAN)
    here = (sibling, me)
    away = [place_on(chips, c) for c in FIRST for chips in (2, 1, 3)]
    everywhere = [*away, *here]

    def share_key(h, part, steps=everywhere):
        share(k_ref, h, kv.at[0, h, own], x_send.at[0, h], x_recv.at[0, h, part], steps)

    def share_value(h, part, steps=everywhere):
        share(v_ref, h, kv.at[1, h, own], x_send.at[1, h], x_recv.at[1, h, part], steps)

    def share_query(h, part):
        share(q_ref, h, qb.at[h], q_send.at[h], q_recv.at[h, part], everywhere)

    share_key(0, 0, here)
    share_value(0, 0, here)
    share_key(0, 1, away)
    share_value(0, 1, away)
    share(q_ref, 0, qb.at[0], q_send.at[0], chip_recv.at[0], here)
    for h in SPLIT:
        @pl.when(x < BACK[h])
        def _():
            share_query(h, 0)
            share_key(h, 0)
            share_value(h, 0)

        @pl.when(x >= BACK[h])
        def _():
            share_key(h, 1)
            share_value(h, 1)
            share_query(h, 1)

    for chips in (1, 3, 2):
        share(q_ref, 0, qb.at[0], q_send.at[0], chip_recv.at[chips], [place_on(chips, c) for c in FIRST])

    def await_bytes(ref, sem):
        pltpu.make_async_copy(ref, ref, sem).wait()

    def forward(t, h):
        first = BACK[h] * BLK
        return remote(kv.at[t, h, pl.ds(SPAN + first, SPAN - first)], kv.at[t, h, pl.ds(first, SPAN - first)],
                      y_send.at[t, h], y_recv.at[t, h], after)

    def forward_block(t, i):
        rows = pl.ds(pl.multiple_of(i * BLK, BLK), BLK)
        return remote(kv.at[t, 0, own].at[rows], kv.at[t, 0, rows], y_send.at[t, 0], y_recv.at[t, 0], after)

    def backward(h):
        first = pl.ds(0, BACK[h] * BLK)
        return remote(qb.at[h, first], qn.at[h, first], qb_send.at[h], qb_recv.at[h], before)

    def partial_out(h, i):
        return remote(on.at[h, pl.ds(i * BLK, BLK)], op.at[h, pl.ds(i * BLK, BLK)],
                      p_send.at[h, i], p_recv.at[h, i], after)

    def partial_stats(h, i):
        return remote(sn.at[h, i], sp.at[h, i], s_send.at[h, i], s_recv.at[h, i], after)

    def table_forward():
        return remote(table.at[pl.ds(ROW, ROW)], table.at[pl.ds(0, ROW)], idf_send, idf_recv, after)

    def table_backward():
        return remote(table.at[pl.ds(ROW, ROW)], table.at[pl.ds(2 * ROW, ROW)], idb_send, idb_recv, before)

    def when(condition, *actions):
        @pl.when(condition)
        def _():
            for action in actions:
                action()

    def first_rows(h):
        return pl.ds(0, BACK[h] * BLK)

    def last_rows(h):
        return pl.ds(BACK[h] * BLK, SPAN - BACK[h] * BLK)

    def pass_on(t, h):
        await_bytes(kv.at[t, h, last_rows(h)], x_recv.at[t, h, 1])
        when(has_next, lambda: forward(t, h).start())

    def pass_own(t):
        await_bytes(kv.at[t, 0, pl.ds(0, BLK)], x_recv.at[t, 0, 0])
        when(has_next, lambda: forward_block(t, x).start())

    def pass_rest(t):
        await_bytes(kv.at[t, 0, pl.ds(0, SPAN - BLK)], x_recv.at[t, 0, 1])
        when(has_next, *[lambda n=n: forward_block(t, (x + n) % ROW).start() for n in (1, 3, 2)])

    def pass_back(h):
        await_bytes(qb.at[h, first_rows(h)], q_recv.at[h, 0])
        when(has_prev, lambda: backward(h).start())

    def await_first(h):
        for t in range(2):
            await_bytes(kv.at[t, h, first_rows(h)], x_recv.at[t, h, 0])

    def await_last(h):
        await_bytes(qb.at[h, last_rows(h)], q_recv.at[h, 1])

    for copy in id_copies:
        copy.wait()
    own_ids.wait()
    when(has_next, lambda: table_forward().start())
    when(has_prev, lambda: table_backward().start())

    def pair(query_slot, key_slot):
        d = query_slot - key_slot
        if d < 0 or d > WIN:
            return jnp.full((BLK, BLK), MASKED, jnp.float32)
        about = table[query_slot]
        column = jnp.transpose(about.astype(jnp.float32))
        there = table[key_slot].astype(jnp.float32)
        allowed = (there[0:1] == column[:, 0:1]) & (there[1:2] <= column[:, 1:2])
        if d:
            kind = about[1 + d:2 + d]
            if key_slot < ROW:
                kind = jnp.where(has_prev, kind, 0)
            allowed = (kind == 2) | ((kind == 1) & allowed)
        return jnp.where(allowed, 0.0, MASKED)

    def terms(ref, i, query_slot, slots):
        for n, slot in enumerate(slots):
            ref[i, :, n * BLK:(n + 1) * BLK] = pair(query_slot, slot)

    def score(queries, keys, term):
        return lax.dot_general(
            queries, keys, (((1,), (1,)), ((), ())), preferred_element_type=jnp.float32) + term

    def weigh(scores):
        highest = jnp.max(scores, axis=1, keepdims=True)
        weights = jnp.exp2((scores - highest) * FACTOR)
        return highest, jnp.sum(weights, axis=1, keepdims=True), weights.astype(jnp.bfloat16)

    def blend(weights, values):
        return jnp.dot(weights, values, preferred_element_type=jnp.float32)

    def block(i):
        return pl.ds(i * BLK if isinstance(i, int) else pl.multiple_of(i * BLK, BLK), BLK)

    def window(h, i):
        if isinstance(i, int) and i < BACK[h]:
            return pl.ds(BACK[h] * BLK, (ROW + 1 + i - BACK[h]) * BLK)
        return pl.ds(block(i).start, WINDOW)

    def partial(h):
        def rows(i):
            return pl.ds(SPAN + i * BLK, (BACK[h] - i) * BLK)

        def scores(i):
            return score(qn[h, block(i)], kv[0, h, rows(i)], bias_n[i, :, i * BLK:BACK[h] * BLK])

        following = scores(BACK[h] - 1)
        for i in reversed(range(BACK[h])):
            current = following
            if i:
                following = scores(i - 1)
            highest, total, weights = weigh(current)
            on[h, block(i)] = blend(weights, kv[1, h, rows(i)]).astype(jnp.bfloat16)
            lane = lax.broadcasted_iota(jnp.int32, (BLK, HD), 1)
            sn[h, i] = jnp.transpose(jnp.where(lane == 0, highest, total))[0:8]
            partial_out(h, i).start()
            partial_stats(h, i).start()

    def give_back(h, i):
        columns = pl.ds(pl.multiple_of(HD * (HEADS * me + h), HD), HD)
        for place in (2 * i + 1, 2 * i):
            rows = ob.at[h, pl.ds(pl.multiple_of(SHARE * place, SHARE), SHARE)]

            @pl.when(me != place)
            def _():
                remote(rows, o_ref.at[:, columns], o_send.at[h], o_recv.at[h], device(place)).start()

            @pl.when(me == place)
            def _():
                pltpu.make_async_copy(rows, o_ref.at[:, columns], o_recv.at[h]).start()

    def weigh_all(h):
        def scores(i):
            first = (BACK[h] - i) * BLK if i < BACK[h] else 0
            return score(qb[h, block(i)], kv[0, h, window(h, i)], bias[i, :, first:])

        following = scores(0)
        for i in range(ROW):
            current = following
            if i + 1 < ROW:
                following = scores(i + 1)
            tops[i], totals[i], weights_of[i, :, 0:window(h, i).size] = weigh(current)

    def blend_all(h):
        for i in range(ROW):
            rows = window(h, i)
            outs[i] = blend(weights_of[i, :, 0:rows.size], kv[1, h, rows])

    def merge(h):
        def body(n, carry):
            i = (x + jnp.where(n < 2, 2 - n, (n + 1) % ROW)) % ROW

            @pl.when(has_prev & (i < BACK[h]))
            def _():
                partial_out(h, i).wait_recv()
                partial_stats(h, i).wait_recv()

            stats = jnp.transpose(sp[h, i])
            highest, other = tops[i], stats[:, 0:1]
            top = jnp.maximum(highest, other)
            here, there = jnp.exp2((highest - top) * FACTOR), jnp.exp2((other - top) * FACTOR)
            total = totals[i] * here + stats[:, 1:2] * there
            out = outs[i] * here + op[h, block(i)].astype(jnp.float32) * there
            ob[h, block(i)] = (out / total).astype(jnp.bfloat16)
            give_back(h, i)
            return carry

        lax.fori_loop(0, ROW, body, 0)

    def attend(*distances):
        def scores(chips):
            i = (x + ROW - chips) % ROW
            await_bytes(qb.at[0, block(i)], chip_recv.at[chips])
            return i, score(qb[0, block(i)], kv[0, 0, window(0, i)], bias[i])

        following = scores(distances[0])
        for n in range(len(distances)):
            i, current = following
            if n + 1 < len(distances):
                following = scores(distances[n + 1])
            _, total, weights = weigh(current)
            out = blend(weights, kv[1, 0, window(0, i)])
            ob[0, block(i)] = (out / total).astype(jnp.bfloat16)
            give_back(0, i)

    def await_keys(h):
        when(has_prev, lambda: forward(0, h).wait_recv())

    def await_values(h):
        when(has_prev, lambda: forward(1, h).wait_recv())

    def next_part(h):
        @pl.when(has_next)
        def _():
            backward(h).wait_recv()
            partial(h)

    pass_own(0)
    pass_own(1)
    pass_rest(0)
    when(has_prev, lambda: table_forward().wait_recv())
    for i in range(ROW):
        terms(bias, i, ROW + i, range(i, ROW + i + 1))

    @pl.when(has_next)
    def _():
        table_backward().wait_recv()
        for i in range(MOST):
            terms(bias_n, i, 2 * ROW + i, range(ROW, ROW + MOST))

    pass_rest(1)
    pass_back(1)
    pass_on(0, 1)
    pass_on(1, 1)
    await_first(1)
    next_part(1)
    pass_back(2)
    pass_on(0, 2)
    await_last(1)
    await_keys(1)
    weigh_all(1)
    pass_on(1, 2)
    await_values(1)
    blend_all(1)
    await_keys(0)
    await_values(0)
    await_first(2)
    next_part(2)
    merge(1)
    attend(1, 3, 2)
    await_last(2)
    await_keys(2)
    weigh_all(2)
    await_values(2)
    blend_all(2)
    merge(2)
    attend(0)

    sent = (TEAM - 1) * SHARE
    for h in range(HEADS):
        for t in range(2):
            await_bytes(kv.at[t, h, pl.ds(0, sent)], x_send.at[t, h])
        await_bytes(qb.at[h, pl.ds(0, sent)], q_send.at[h])

    @pl.when(has_next)
    def _():
        table_forward().wait_send()
        for h in range(HEADS):
            forward(0, h).wait_send()
            forward(1, h).wait_send()
        for h in SPLIT:
            for i in range(BACK[h]):
                partial_out(h, i).wait_send()
                partial_stats(h, i).wait_send()

    @pl.when(has_prev)
    def _():
        table_backward().wait_send()
        for h in SPLIT:
            backward(h).wait_send()

    for h in range(HEADS):
        await_bytes(qb.at[h, pl.ds(0, sent)], o_send.at[h])
        await_bytes(qb.at[h], o_recv.at[h])


def shards(queries, keys, values, clip_ids, group_ids, pair_kinds):
    hbm = pl.BlockSpec(memory_space=pl.ANY)
    vmem = pl.BlockSpec(memory_space=pltpu.VMEM)
    dma = pltpu.SemaphoreType.DMA
    bf16 = jnp.bfloat16
    return pl.pallas_call(
        kernel,
        out_shape=jax.ShapeDtypeStruct(queries.shape, bf16),
        in_specs=[hbm, hbm, hbm, vmem, vmem, pl.BlockSpec(memory_space=pltpu.SMEM)],
        out_specs=hbm,
        scratch_shapes=[
            pltpu.VMEM((8, BLK), jnp.int32),
            pltpu.VMEM((3 * ROW, 8, BLK), jnp.int32),
            pltpu.VMEM((2, HEADS, 2 * SPAN, HD), bf16),
            pltpu.VMEM((HEADS, SPAN, HD), bf16),
            pltpu.VMEM((HEADS, SPAN, HD), bf16),
            pltpu.VMEM((HEADS, MOST * BLK, HD), bf16),
            pltpu.VMEM((HEADS, MOST * BLK, HD), bf16),
            pltpu.VMEM((HEADS, MOST, 8, BLK), jnp.float32),
            pltpu.VMEM((HEADS, SPAN, HD), bf16),
            pltpu.VMEM((HEADS, ROW, 8, BLK), jnp.float32),
            pltpu.VMEM((ROW, BLK, WINDOW), jnp.float32),
            pltpu.VMEM((MOST, BLK, MOST * BLK), jnp.float32),
            pltpu.VMEM((ROW, BLK, 1), jnp.float32),
            pltpu.VMEM((ROW, BLK, 1), jnp.float32),
            pltpu.VMEM((ROW, BLK, HD), jnp.float32),
            pltpu.VMEM((ROW, BLK, WINDOW), bf16),
            dma((3,)), dma((4,)), dma, dma, dma, dma,
            dma((2, HEADS)), dma((2, HEADS, 2)), dma((HEADS,)), dma((HEADS, 2)),
            dma((2, HEADS)), dma((2, HEADS)), dma((ROW,)), dma((HEADS,)), dma((HEADS,)),
            dma((HEADS, MOST)), dma((HEADS, MOST)), dma((HEADS, MOST)), dma((HEADS, MOST)), dma((HEADS,)), dma((HEADS,)),
        ],
        compiler_params=pltpu.CompilerParams(
            collective_id=0, has_side_effects=True, vmem_limit_bytes=53 * 1024 * 1024),
    )(queries, keys, values, clip_ids.reshape(1, BLK), group_ids.reshape(1, BLK), pair_kinds)


def solution(mesh):
    tokens = P(("ctx", "head"), None)
    return jax.shard_map(
        shards, mesh=mesh, in_specs=(tokens, tokens, tokens, P("ctx"), P("ctx"), P("ctx", None)),
        out_specs=tokens, check_vma=False)
```
